128 devices in a mesh: ctx: 4 (over y), head: 32 (over x, z, core).
Axes of the slice: x: 4, y: 4, z: 4, core: 2. Of those that a mesh axis runs over, the one named last changes fastest.
Arguments:
- queries: bfloat16 [16384, 4096], P(('ctx', 'head')), may hold values from -24 to 24
- keys: bfloat16 [16384, 1024], P(('ctx', 'head')), may hold values from -10 to 10
- values: bfloat16 [16384, 1024], P(('ctx', 'head')), may hold values from -6 to 6
Outputs:
- attended: bfloat16 [16384, 4096], P(('ctx', 'head'))
The draws below stay inside these ranges and needn't reach their ends.
All inputs are finite; a program needn't handle non-finite values.
Results may differ from the reference program's by a relative error of at most 0.0049.
Values may be sent and summed in bfloat16 or wider, within the bound.
A program may use at most 192 MiB of HBM per device.

```python
import jax
import jax.numpy as jnp
from jax import lax

HQ = 32
KEY_VALUE_HEADS = 8
HEAD_WIDTH = 128
QUERY_PER_KEY = 4
TILE_ROWS = 1024
SEQUENCE_TOKENS = 16384


def draw_keys(key, part):
    key = jax.random.fold_in(key, 1)
    start_offset = 2.5 * jnp.clip(jax.random.normal(key, (SEQUENCE_TOKENS, KEY_VALUE_HEADS, HEAD_WIDTH), jnp.float32), -4.0, 4.0)
    return start_offset.reshape(SEQUENCE_TOKENS, KEY_VALUE_HEADS * HEAD_WIDTH).astype(jnp.bfloat16)


def draw_queries(key, part):
    key = jax.random.fold_in(key, 2)
    start_offset = jnp.clip(jax.random.normal(key, (SEQUENCE_TOKENS, KEY_VALUE_HEADS, QUERY_PER_KEY, HEAD_WIDTH), jnp.float32), -4.0, 4.0)
    return start_offset.reshape(SEQUENCE_TOKENS, HQ * HEAD_WIDTH).astype(jnp.bfloat16)


def block_scale(stream_key, dims, cuts, low, top_value):
    def one(position, shards_of):
        heights = jax.random.uniform(jax.random.fold_in(jax.random.fold_in(stream_key, 6), position), (shards_of,), jnp.float32, low / len(cuts), top_value / len(cuts))
        return jnp.repeat(jnp.exp(heights), dims[position] // shards_of).reshape((-1,) + (1,) * (len(dims) - position - 1))

    gain = one(*cuts[0])
    for cut in cuts[1:]:
        gain = gain * one(*cut)
    return gain


def noise(rng, extent, deviation, bound, shards=(), kind=jnp.bfloat16):
    result = jax.random.normal(rng, extent, jnp.float32) * deviation
    if len(shards) > 0:
        result = block_scale(rng, extent, shards, -0.22, 0.18) * result
    return jnp.clip(result, min=-bound, max=bound).astype(kind)


def setup_inputs(seed: int = 0) -> dict:
    arg_keys = jax.random.split(jax.random.key(seed), 4)
    queries = draw_queries(jax.random.fold_in(arg_keys[3], 71), 0)
    keys = draw_keys(jax.random.fold_in(arg_keys[3], 71), 0)
    values = noise(arg_keys[2], (SEQUENCE_TOKENS, KEY_VALUE_HEADS * HEAD_WIDTH), 1.0, 6.0, ((0, 128),))
    return {"queries": queries, "keys": keys, "values": values}


def reference(queries, keys, values):
    every_query = queries.astype(jnp.float32).reshape(SEQUENCE_TOKENS, KEY_VALUE_HEADS, QUERY_PER_KEY, HEAD_WIDTH)
    every_key = keys.astype(jnp.float32).reshape(SEQUENCE_TOKENS, KEY_VALUE_HEADS, HEAD_WIDTH)
    every_value = values.astype(jnp.float32).reshape(SEQUENCE_TOKENS, KEY_VALUE_HEADS, HEAD_WIDTH)
    count_of_tiles = SEQUENCE_TOKENS // TILE_ROWS
    positions = jnp.arange(SEQUENCE_TOKENS, dtype=jnp.int32)
    scale = HEAD_WIDTH ** -0.5

    def output_of_tile(index):
        kv_head = (index // count_of_tiles).astype(jnp.int32)
        q_start = ((index % count_of_tiles) * TILE_ROWS).astype(jnp.int32)
        q_rows = lax.dynamic_slice_in_dim(every_query, q_start, TILE_ROWS, 0)
        q_rows = lax.dynamic_index_in_dim(q_rows, kv_head, 1, keepdims=False)
        k_head = lax.dynamic_index_in_dim(every_key, kv_head, 1, keepdims=False)
        v_head = lax.dynamic_index_in_dim(every_value, kv_head, 1, keepdims=False)
        scores = jnp.einsum("rgd,td->rgt", q_rows, k_head, precision=lax.Precision.HIGHEST) * scale
        allowed = (q_start + jnp.arange(TILE_ROWS, dtype=jnp.int32))[:, None, None] >= positions[None, None, :]
        scores = jnp.where(allowed, scores, jnp.float32(-1e30))
        row_max = jnp.max(scores, axis=-1, keepdims=True)
        weights = jnp.where(allowed, jnp.exp(scores - row_max), jnp.float32(0.0))
        totals = jnp.sum(weights, axis=-1)
        rounded = lax.optimization_barrier(weights.astype(jnp.bfloat16)).astype(jnp.float32)
        output = jnp.einsum("rgt,td->rgd", rounded, v_head, precision=lax.Precision.HIGHEST) / totals[..., None]
        return output.reshape(TILE_ROWS, QUERY_PER_KEY * HEAD_WIDTH).astype(jnp.bfloat16)

    context_portions = lax.map(output_of_tile, jnp.arange(KEY_VALUE_HEADS * count_of_tiles, dtype=jnp.int32))
    context_portions = context_portions.reshape(KEY_VALUE_HEADS, count_of_tiles, TILE_ROWS, QUERY_PER_KEY * HEAD_WIDTH).transpose(1, 2, 0, 3)
    return context_portions.reshape(SEQUENCE_TOKENS, HQ * HEAD_WIDTH)
```

```python
import jax
import jax.numpy as jnp
from jax import lax
from jax.experimental import pallas as pl
from jax.experimental.pallas import tpu as pltpu
from jax.sharding import PartitionSpec as P

BLOCK = 128
WIDTH = 128
CHUNK = 1024
GROUP = 4 * WIDTH
SLOTS = 8
LOG2_SCALE = WIDTH**-0.5 * 1.4426950408889634
MESH = pl.DeviceIdType.MESH
F32 = jnp.float32
BF16 = jnp.bfloat16


def kernel(
    q_ref, k_ref, v_ref, out_ref,
    kv, vt, q_in, q_pair, peak, total, acc, score_a, score_b, o_buf,
    local_sem, home_send, home_recv, x_send, x_recv, z_send, z_recv, far_send, far_recv,
    core_send, core_recv, out_send, out_recv,
):
    y = lax.axis_index("ctx")
    head = lax.axis_index("head")
    x, zc = head // 8, lax.rem(head, 8)
    z, c = zc // 2, lax.rem(zc, 2)
    low = lax.min(x, 3 - x)
    x_mate = x + 1 - 2 * lax.rem(x, 2)
    z_up, z_down, z_far = lax.rem(z + 1, 4), lax.rem(z + 3, 4), lax.rem(z + 2, 4)
    my_slot = 2 * y + x // 2
    my_head = 2 * y + x // 2

    def at(ctx, x_, z_, c_):
        return (ctx, x_ * 8 + z_ * 2 + c_)

    homes = []
    for dy in range(4):
        for dx in range(2):
            homes.append((lax.rem(y + dy, 4), x if dx == 0 else 3 - x))
    mate, up, down, twin = at(y, x_mate, z, c), at(y, x, z_up, c), at(y, x, z_down, c), at(y, x, z, 1 - c)

    barrier = pltpu.get_barrier_semaphore()
    for hy, hx in homes[1:]:
        pl.semaphore_signal(barrier, inc=1, device_id=at(hy, hx, z, c), device_id_type=MESH)
    for other in (mate, up, down, twin):
        pl.semaphore_signal(barrier, inc=1, device_id=other, device_id_type=MESH)
    pl.semaphore_wait(barrier, 11)

    home, along_x, along_z = (home_send, home_recv), (x_send, x_recv), (z_send, z_recv)
    far, core = (far_send, far_recv), (core_send, core_recv)
    sent = []

    def send(src, dst, sems, index, device, recv_index=None):
        send_sem, recv_sem = sems
        pltpu.make_async_remote_copy(
            src_ref=src,
            dst_ref=dst,
            send_sem=send_sem.at[index],
            recv_sem=recv_sem.at[index if recv_index is None else recv_index],
            device_id=device,
            device_id_type=MESH,
        ).start()
        sent.append((send_sem, index, src.shape))

    def arrived(dst, recv_sem):
        pltpu.make_async_remote_copy(
            src_ref=dst, dst_ref=dst, send_sem=local_sem.at[0], recv_sem=recv_sem, device_id=mate, device_id_type=MESH
        ).wait_recv()

    my_chunk = 4 * y + x

    def columns(head_, width):
        return pl.ds(pl.multiple_of(head_ * width, width), width)

    own = [
        pltpu.make_async_copy(k_ref.at[:, columns(my_head, WIDTH)], kv.at[my_chunk, zc, 0], local_sem.at[0]),
        pltpu.make_async_copy(v_ref.at[:, columns(my_head, WIDTH)], kv.at[my_chunk, zc, 1], local_sem.at[1]),
        pltpu.make_async_copy(q_ref.at[:, columns(my_head, GROUP)], q_in.at[my_slot], local_sem.at[2]),
    ]
    for copy in own:
        copy.start()
    for i, (hy, hx) in enumerate(homes):
        if i:
            there, to = 2 * hy + hx // 2, at(hy, hx, z, c)
            send(k_ref.at[:, columns(there, WIDTH)], kv.at[my_chunk, zc, 0], home, (0, i), to, (0, my_slot))
            send(v_ref.at[:, columns(there, WIDTH)], kv.at[my_chunk, zc, 1], home, (1, i), to, (1, my_slot))
    for i, (hy, hx) in enumerate(homes):
        if i:
            there, to = 2 * hy + hx // 2, at(hy, hx, z, c)
            send(q_ref.at[:, columns(there, GROUP)], q_in.at[my_slot], home, (2, i), to, (2, my_slot))

    peak[...] = jnp.full_like(peak, -1e30)
    total[...] = jnp.zeros_like(total)
    acc[...] = jnp.zeros_like(acc)
    for copy in own:
        copy.wait()

    def own_chunk(quarter, i):
        return 4 * quarter + (low if i == 0 else 3 - low)

    mate_low = 1 - low

    def mate_chunk(quarter, i):
        return 4 * quarter + (mate_low if i == 0 else 3 - mate_low)

    def rows(quarter, z_):
        return kv.at[pl.ds(4 * quarter, 4), 2 * z_ + c]

    def gather_1(quarter):
        for i in range(2):
            slot = 2 * quarter + i

            @pl.when(slot != my_slot)
            def _():
                arrived(kv.at[own_chunk(quarter, i), zc, 0], home_recv.at[0, slot])
                arrived(kv.at[own_chunk(quarter, i), zc, 1], home_recv.at[1, slot])

        for i in range(2):
            block = kv.at[own_chunk(quarter, i), zc]
            send(block, block, along_x, (quarter, i), mate)
            send(block, block, along_z, (quarter, 0, i), up)
            send(block, block, along_z, (quarter, 1, i), down)

    def gather_2(quarter):
        for i in range(2):
            block = kv.at[mate_chunk(quarter, i), zc]
            arrived(block, x_recv.at[quarter, i])
            send(block, block, along_z, (quarter, 0, 2 + i), up)
            send(block, block, along_z, (quarter, 1, 2 + i), down)
        send(rows(quarter, z), rows(quarter, z), core, (quarter, 0), twin)

    def gather_3(quarter):
        for way, z_ in ((0, z_down), (1, z_up)):
            for i in range(2):
                arrived(kv.at[own_chunk(quarter, i), 2 * z_ + c], z_recv.at[quarter, way, i])
                arrived(kv.at[mate_chunk(quarter, i), 2 * z_ + c], z_recv.at[quarter, way, 2 + i])
            half = kv.at[pl.ds(4 * quarter, 4), 2 * z_ + c, way]
            send(half, half, far, (quarter, way), up if way == 0 else down)
            send(rows(quarter, z_), rows(quarter, z_), core, (quarter, 1 + way), twin)

    def gather_4(quarter):
        for way in range(2):
            arrived(kv.at[pl.ds(4 * quarter, 4), 2 * z_far + c, way], far_recv.at[quarter, way])
        send(rows(quarter, z_far), rows(quarter, z_far), core, (quarter, 3), twin)

    def gather_5(quarter):
        for i, z_ in enumerate((z, z_down, z_up, z_far)):
            arrived(kv.at[pl.ds(4 * quarter, 4), 2 * z_ + 1 - c], core_recv.at[quarter, i])

    def turn_values(quarter):
        def one(i, _):
            chunk = 4 * quarter + i
            for b in range(8):
                vt[chunk, :, b * BLOCK : (b + 1) * BLOCK] = kv[chunk, b, 1].T
            return 0

        lax.fori_loop(0, 4, one, 0)

    def split_queries(slot):
        for h in range(4):
            scaled = q_in[slot, :, h * WIDTH : (h + 1) * WIDTH].astype(F32) * LOG2_SCALE
            top = scaled.astype(BF16)
            q_pair[slot, h * BLOCK : (h + 1) * BLOCK, :WIDTH] = top
            q_pair[slot, h * BLOCK : (h + 1) * BLOCK, WIDTH:] = (scaled - top.astype(F32)).astype(BF16)

    def score(where, dst):
        slot, chunk = where
        k = kv[chunk, :, 0].reshape(CHUNK, WIDTH)
        dst[...] = lax.dot_general(
            jnp.concatenate([k, k], axis=1), q_pair[slot], (((1,), (1,)), ((), ())), preferred_element_type=F32
        )

    def absorb(where, src, masked=False):
        slot, chunk = where
        s = src[...]
        if masked:
            key = lax.broadcasted_iota(jnp.int32, s.shape, 0)
            token = lax.rem(lax.broadcasted_iota(jnp.int32, s.shape, 1), BLOCK)
            s = jnp.where(key <= token + zc * BLOCK, s, -1e30)
        old = peak[slot]
        new = jnp.maximum(old, jnp.max(s, axis=0, keepdims=True))
        weights = jnp.exp2(s - new)
        rescale = jnp.exp2(old - new)
        peak[slot] = new
        total[slot] = total[slot] * rescale + jnp.sum(weights, axis=0, keepdims=True)
        acc[slot] = acc[slot] * rescale + jnp.dot(vt[chunk], weights.astype(BF16), preferred_element_type=F32)

    def finish(slot, i):
        y_, x_ = slot // 2, (low if i == 0 else 3 - low)
        for h in range(4):
            part = acc[slot, :, h * BLOCK : (h + 1) * BLOCK] / total[slot, :, h * BLOCK : (h + 1) * BLOCK]
            o_buf[slot, :, h * WIDTH : (h + 1) * WIDTH] = part.T.astype(BF16)

        @pl.when(slot != my_slot)
        def _():
            pltpu.make_async_remote_copy(
                src_ref=o_buf.at[slot],
                dst_ref=out_ref.at[:, columns(my_head, GROUP)],
                send_sem=out_send.at[slot],
                recv_sem=out_recv.at[my_head],
                device_id=at(y_, x_, z, c),
                device_id_type=MESH,
            ).start()

        @pl.when(slot == my_slot)
        def _():
            pltpu.make_async_copy(o_buf.at[slot], out_ref.at[:, columns(my_head, GROUP)], local_sem.at[3]).start()

    gather_1(0)
    gather_2(0)
    gather_1(1)
    gather_3(0)
    gather_2(1)
    gather_4(0)
    gather_5(0)
    for slot in range(SLOTS):

        @pl.when(slot != my_slot)
        def _():
            arrived(q_in.at[slot], home_recv.at[2, slot])

        split_queries(slot)

    def both(one, quarter, other, earlier):
        one(quarter)
        other(earlier)

    steps = {
        (0, 1): lambda: gather_3(1),
        (0, 2): lambda: gather_1(2),
        (0, 4): lambda: both(gather_2, 2, gather_4, 1),
        (0, 6): lambda: gather_3(2),
        (0, 7): lambda: gather_1(3),
        (0, 9): lambda: both(gather_2, 3, gather_4, 2),
        (0, 12): lambda: gather_3(3),
        (1, 3): lambda: gather_4(3),
    }

    for p in range(4):
        if p:
            gather_5(p)
        turn_values(p)
        wide = 8 * (3 - p)

        def unit(u, p=p, wide=wide):
            i = u - wide
            second = jnp.where(i >= low, 1, 0)
            slot = jnp.where(u < wide, 2 * (p + 1) + u // 4, 2 * p + second)
            chunk = 4 * p + jnp.where(u < wide, lax.rem(u, 4), i - second * low)
            return slot, chunk

        score(unit(jnp.int32(0)), score_a)

        def pair(i, _, p=p, unit=unit):
            for (phase, step), action in steps.items():
                if phase == p:
                    pl.when(i == step)(action)
            score(unit(2 * i + 1), score_b)
            absorb(unit(2 * i), score_a)
            score(unit(2 * i + 2), score_a)
            absorb(unit(2 * i + 1), score_b)
            return 0

        pairs = (wide + 2) // 2
        lax.fori_loop(0, pairs, pair, 0)
        first, second = (2 * p, 4 * p + low), (2 * p + 1, 4 * p + 3 - low)
        score(first, score_b)
        absorb(unit(jnp.int32(2 * pairs)), score_a)
        score(second, score_a)
        absorb(first, score_b, True)
        finish(2 * p, 0)
        absorb(second, score_a, True)
        finish(2 * p + 1, 1)

    for send_sem, index, shape in sent:
        held = {2: kv.at[0, 0, 0], 3: kv.at[0, 0], 4: kv.at[pl.ds(0, 4), 0]}[len(shape)]
        if shape == (4, BLOCK, WIDTH):
            held = kv.at[pl.ds(0, 4), 0, 0]
        elif shape == (BLOCK, GROUP):
            held = q_in.at[0]
        pltpu.make_async_remote_copy(
            src_ref=held, dst_ref=held, send_sem=send_sem.at[index], recv_sem=local_sem.at[0], device_id=mate,
            device_id_type=MESH,
        ).wait_send()
    for slot in range(SLOTS):
        y_, x_ = slot // 2, (low if slot % 2 == 0 else 3 - low)

        @pl.when(slot != my_slot)
        def _():
            piece = out_ref.at[:, pl.ds(slot * GROUP, GROUP)]
            done = pltpu.make_async_remote_copy(
                src_ref=o_buf.at[slot],
                dst_ref=piece,
                send_sem=out_send.at[slot],
                recv_sem=out_recv.at[slot],
                device_id=at(y_, x_, z, c),
                device_id_type=MESH,
            )
            done.wait_send()
            done.wait_recv()

        @pl.when(slot == my_slot)
        def _():
            pltpu.make_async_copy(o_buf.at[slot], out_ref.at[:, columns(my_head, GROUP)], local_sem.at[3]).wait()


def per_device(queries, keys, values):
    sem = pltpu.SemaphoreType.DMA
    return pl.pallas_call(
        kernel,
        out_shape=jax.ShapeDtypeStruct(queries.shape, BF16),
        in_specs=[pl.BlockSpec(memory_space=pl.ANY)] * 3,
        out_specs=pl.BlockSpec(memory_space=pl.ANY),
        scratch_shapes=[
            pltpu.VMEM((16, 8, 2, BLOCK, WIDTH), BF16),
            pltpu.VMEM((16, WIDTH, CHUNK), BF16),
            pltpu.VMEM((SLOTS, BLOCK, GROUP), BF16),
            pltpu.VMEM((SLOTS, 4 * BLOCK, 2 * WIDTH), BF16),
            pltpu.VMEM((SLOTS, 1, 4 * BLOCK), F32),
            pltpu.VMEM((SLOTS, 1, 4 * BLOCK), F32),
            pltpu.VMEM((SLOTS, WIDTH, 4 * BLOCK), F32),
            pltpu.VMEM((CHUNK, 4 * BLOCK), F32),
            pltpu.VMEM((CHUNK, 4 * BLOCK), F32),
            pltpu.VMEM((SLOTS, BLOCK, GROUP), BF16),
            sem((4,)),
            sem((3, 8)), sem((3, 8)),
            sem((4, 2)), sem((4, 2)),
            sem((4, 2, 4)), sem((4, 2, 4)),
            sem((4, 2)), sem((4, 2)),
            sem((4, 4)), sem((4, 4)),
            sem((8,)), sem((8,)),
        ],
        compiler_params=pltpu.CompilerParams(
            collective_id=0, has_side_effects=True, vmem_limit_bytes=56 * 2**20
        ),
        name="causal_attention",
    )(queries, keys, values)


def solution(mesh):
    spec = P(("ctx", "head"), None)
    return jax.shard_map(per_device, mesh=mesh, in_specs=(spec, spec, spec), out_specs=spec, check_vma=False)
```

```python
import jax
import jax.numpy as jnp
from jax import lax
from jax.experimental import pallas as pl
from jax.experimental.pallas import tpu as pltpu
from jax.sharding import PartitionSpec as P

BLOCK = 128
WIDTH = 128
GROUP = 4 * WIDTH
ROWS = 4 * BLOCK
CHUNK = 1024
PART = 2048
SPAN = 256
SLOTS = 8
UNITS = 28
LOG2_SCALE = WIDTH**-0.5 * 1.4426950408889634
MESH = pl.DeviceIdType.MESH
F32 = jnp.float32
BF16 = jnp.bfloat16


def kernel(
    q_ref, k_ref, v_ref, out_ref,
    kv, v_raw, v_turned, q_in, q_pair, peak, total, acc, score_a, score_b, top_a, top_b, o_buf,
    local_sem, home_send, home_recv, x_send, x_recv, z_send, z_recv, far_send, far_recv,
    core_send, core_recv, out_send, out_recv,
):
    y = lax.axis_index("ctx")
    head = lax.axis_index("head")
    x, zc = head // 8, lax.rem(head, 8)
    z, c = zc // 2, lax.rem(zc, 2)
    low = lax.min(x, 3 - x)
    half = x // 2
    x_mate = x + 1 - 2 * lax.rem(x, 2)
    z_up, z_down, z_far = lax.rem(z + 1, 4), lax.rem(z + 3, 4), lax.rem(z + 2, 4)
    my_slot = 2 * y + half
    my_head = 2 * y + half

    def at(ctx, x_, z_, c_):
        return (ctx, x_ * 8 + z_ * 2 + c_)

    homes = []
    for dy in (2, 1, 3, 0):
        for dx in (1, 0):
            homes.append((lax.rem(y + dy, 4), x if dx == 0 else 3 - x))
    homes = homes[:-1]
    mate, up, down, twin = at(y, x_mate, z, c), at(y, x, z_up, c), at(y, x, z_down, c), at(y, x, z, 1 - c)

    barrier = pltpu.get_barrier_semaphore()
    for hy, hx in homes:
        pl.semaphore_signal(barrier, inc=1, device_id=at(hy, hx, z, c), device_id_type=MESH)
    for other in (mate, up, down, twin):
        pl.semaphore_signal(barrier, inc=1, device_id=other, device_id_type=MESH)

    def columns(head_, width):
        return pl.ds(pl.multiple_of(head_ * width, width), width)

    my_chunk = 4 * y + half
    load_v = pltpu.make_async_copy(v_ref, v_raw, local_sem.at[0])
    load_v.start()
    own = [
        pltpu.make_async_copy(k_ref.at[:, columns(my_head, WIDTH)], kv.at[my_chunk, zc, 0], local_sem.at[1]),
        pltpu.make_async_copy(q_ref.at[:, columns(my_head, GROUP)], q_in.at[my_slot], local_sem.at[2]),
    ]
    for copy in own:
        copy.start()
    peak[...] = jnp.full_like(peak, -1e30)
    total[...] = jnp.zeros_like(total)
    acc[...] = jnp.zeros_like(acc)
    load_v.wait()
    for h in range(8):
        v_turned[h] = v_raw[:, h * WIDTH : (h + 1) * WIDTH].T
    own.append(pltpu.make_async_copy(v_turned.at[my_head], kv.at[my_chunk, zc, 1], local_sem.at[3]))
    own[-1].start()

    pl.semaphore_wait(barrier, 11)

    home, along_x, along_z = (home_send, home_recv), (x_send, x_recv), (z_send, z_recv)
    far, core = (far_send, far_recv), (core_send, core_recv)
    sent = []

    def send(src, dst, sems, index, device, recv_index=None):
        send_sem, recv_sem = sems
        pltpu.make_async_remote_copy(
            src_ref=src,
            dst_ref=dst,
            send_sem=send_sem.at[index],
            recv_sem=recv_sem.at[index if recv_index is None else recv_index],
            device_id=device,
            device_id_type=MESH,
        ).start()
        sent.append((send_sem, index, src.shape))

    def arrived(dst, recv_sem):
        pltpu.make_async_remote_copy(
            src_ref=dst, dst_ref=dst, send_sem=local_sem.at[0], recv_sem=recv_sem, device_id=mate, device_id_type=MESH
        ).wait_recv()

    for i, (hy, hx) in enumerate(homes):
        there, to = 2 * hy + hx // 2, at(hy, hx, z, c)
        send(k_ref.at[:, columns(there, WIDTH)], kv.at[my_chunk, zc, 0], home, (0, i), to, (0, my_slot))
        send(v_turned.at[there], kv.at[my_chunk, zc, 1], home, (1, i), to, (1, my_slot))
    for i, (hy, hx) in enumerate(homes):
        there, to = 2 * hy + hx // 2, at(hy, hx, z, c)
        send(q_ref.at[:, columns(there, GROUP)], q_in.at[my_slot], home, (2, i), to, (2, my_slot))

    for copy in own:
        copy.wait()

    def pair(quarter, m, z_, c_=c):
        return kv.at[pl.ds(4 * quarter + 2 * m, 2), 2 * z_ + c_]

    def half_pair(quarter, m, z_, way):
        return kv.at[pl.ds(4 * quarter + 2 * m, 2), 2 * z_ + c, way]

    def to_mate(quarter):
        for i in range(2):
            slot = 2 * quarter + i

            @pl.when(slot != my_slot)
            def _():
                arrived(kv.at[4 * quarter + i, zc, 0], home_recv.at[0, slot])
                arrived(kv.at[4 * quarter + i, zc, 1], home_recv.at[1, slot])

        send(pair(quarter, 0, z), pair(quarter, 1, z), along_x, (quarter,), mate)
        send(pair(quarter, 0, z), pair(quarter, 0, z), core, (quarter, 0, 0), twin)

    def to_ring(quarter, m):
        if m:
            arrived(pair(quarter, 1, z), x_recv.at[quarter])
            send(pair(quarter, 1, z), pair(quarter, 1, z), core, (quarter, 1, 0), twin)
        send(pair(quarter, m, z), pair(quarter, m, z), along_z, (quarter, m, 0), up)
        send(pair(quarter, m, z), pair(quarter, m, z), along_z, (quarter, m, 1), down)

    def round_ring(quarter, m):
        for way, z_ in ((0, z_down), (1, z_up)):
            arrived(pair(quarter, m, z_), z_recv.at[quarter, m, way])
            part = half_pair(quarter, m, z_, way)
            send(part, part, far, (quarter, m, way), up if way == 0 else down)
            send(pair(quarter, m, z_), pair(quarter, m, z_), core, (quarter, m, 1 + way), twin)

    def from_far(quarter, m):
        for way in range(2):
            arrived(half_pair(quarter, m, z_far, way), far_recv.at[quarter, m, way])
        send(pair(quarter, m, z_far), pair(quarter, m, z_far), core, (quarter, m, 3), twin)

    def from_twin(quarter, m):
        for i, z_ in enumerate((z, z_down, z_up, z_far)):
            arrived(pair(quarter, m, z_, 1 - c), core_recv.at[quarter, m, i])

    def split_queries(slot):
        @pl.when(slot != my_slot)
        def _():
            arrived(q_in.at[slot], home_recv.at[2, slot])

        for h in range(4):
            scaled = q_in[slot, :, h * WIDTH : (h + 1) * WIDTH].astype(F32) * LOG2_SCALE
            first = scaled.astype(BF16)
            q_pair[slot, h * BLOCK : (h + 1) * BLOCK, :WIDTH] = first
            q_pair[slot, h * BLOCK : (h + 1) * BLOCK, WIDTH:] = (scaled - first.astype(F32)).astype(BF16)

    def parts(chunks):
        blocks = [(chunk, b) for chunk in chunks for b in range(8)]
        return [blocks[i : i + PART // BLOCK] for i in range(0, len(blocks), PART // BLOCK)]

    def work(ahead, behind):
        ahead_parts = parts(ahead[1]) if ahead else []
        behind_parts = parts(behind[1]) if behind else []
        for start in range(0, ROWS, SPAN):
            columns_ = slice(start, start + SPAN)
            if behind:
                slot, _, src, src_top = behind
                old = peak[slot, :, columns_]
                new = jnp.maximum(old, jnp.max(src_top[:, columns_], axis=0, keepdims=True))
                rescale = jnp.exp2(old - new)
                peak[slot, :, columns_] = new
                sums, mixture = total[slot, :, columns_] * rescale, None
            highest = None
            for i in range(max(len(ahead_parts), len(behind_parts))):
                if i < len(ahead_parts):
                    slot_, chunks_, dst, dst_top, masked = ahead
                    k = jnp.concatenate([kv[chunk, b, 0] for chunk, b in ahead_parts[i]], axis=0)
                    rows = slice(i * PART, i * PART + k.shape[0])
                    s = lax.dot_general(
                        jnp.concatenate([k, k], axis=1), q_pair[slot_, columns_], (((1,), (1,)), ((), ())),
                        preferred_element_type=F32,
                    )
                    if masked and rows.stop > CHUNK * (len(chunks_) - 1):
                        past = rows.start - CHUNK * (len(chunks_) - 1)
                        key = past + lax.broadcasted_iota(jnp.int32, s.shape, 0)
                        token = lax.rem(lax.broadcasted_iota(jnp.int32, s.shape, 1), BLOCK)
                        s = jnp.where(key <= token + zc * BLOCK, s, -1e30)
                    dst[rows, columns_] = s
                    best = jnp.max(s.reshape(-1, 8, SPAN), axis=0)
                    highest = best if highest is None else jnp.maximum(highest, best)
                if i < len(behind_parts):
                    rows = slice(i * PART, i * PART + BLOCK * len(behind_parts[i]))
                    weights = jnp.exp2(src[rows, columns_] - new)
                    sums = sums + jnp.sum(weights.reshape(-1, 8, SPAN), axis=0)
                    v = jnp.concatenate([kv[chunk, b, 1] for chunk, b in behind_parts[i]], axis=1)
                    term = jnp.dot(v, weights.astype(BF16), preferred_element_type=F32)
                    mixture = term if mixture is None else mixture + term
            if ahead:
                dst_top[:, columns_] = highest
            if behind:
                total[slot, :, columns_] = sums
                acc[slot, :, columns_] = acc[slot, :, columns_] * rescale + mixture

    def finish(slot):
        for h in range(4):
            columns_ = slice(h * BLOCK, (h + 1) * BLOCK)
            part = acc[slot, :, columns_] / jnp.sum(total[slot, :, columns_], axis=0, keepdims=True)
            o_buf[slot, :, h * WIDTH : (h + 1) * WIDTH] = part.T.astype(BF16)

        @pl.when(slot != my_slot)
        def _():
            pltpu.make_async_remote_copy(
                src_ref=o_buf.at[slot],
                dst_ref=out_ref.at[:, columns(my_head, GROUP)],
                send_sem=out_send.at[slot],
                recv_sem=out_recv.at[my_head],
                device_id=at(slot // 2, low + lax.rem(slot, 2) * (3 - 2 * low), z, c),
                device_id_type=MESH,
            ).start()

        @pl.when(slot == my_slot)
        def _():
            pltpu.make_async_copy(o_buf.at[slot], out_ref.at[:, columns(my_head, GROUP)], local_sem.at[0]).start()

    to_mate(0)
    to_ring(0, 0)
    to_mate(1)
    to_mate(2)
    to_mate(3)
    round_ring(0, 0)
    to_ring(0, 1)
    from_far(0, 0)
    to_ring(1, 0)
    for slot in range(SLOTS):
        split_queries(slot)
    from_twin(0, 0)

    def unit(u):
        p = jnp.where(u >= 13, 1, 0) + jnp.where(u >= 22, 1, 0) + jnp.where(u >= 27, 1, 0)
        i = u - (13 * p - 2 * p * (p - 1))
        later = 2 * (3 - p)
        kind = jnp.where(i >= later, 1, 0) + jnp.where(i >= 2 * later, 1, 0)
        slot = jnp.where(kind == 2, 2 * p + 1, 2 * (p + 1) + i - kind * later)
        one = 4 * p + 2 * lax.rem(kind, 2)
        return slot, (one, one + 1 + lax.div(kind, 2))

    steps = {
        0: [(round_ring, 0, 1)],
        1: [(round_ring, 1, 0), (to_ring, 1, 1)],
        2: [(from_far, 0, 1), (from_twin, 0, 1)],
        3: [(to_ring, 2, 0), (from_far, 1, 0)],
        4: [(round_ring, 1, 1), (to_ring, 2, 1)],
        5: [(round_ring, 2, 0), (from_far, 1, 1), (to_ring, 3, 0)],
        6: [(from_twin, 1, 0), (round_ring, 2, 1), (to_ring, 3, 1)],
        7: [(from_far, 2, 0), (from_twin, 1, 1)],
        8: [(round_ring, 3, 0), (from_far, 2, 1)],
        9: [(round_ring, 3, 1)],
        10: [(from_far, 3, 0), (from_twin, 2, 0)],
        11: [(from_far, 3, 1), (from_twin, 2, 1)],
        12: [(from_twin, 3, 0), (from_twin, 3, 1)],
    }

    def do(actions):
        def run():
            for action, quarter, m in actions:
                action(quarter, m)

        return run

    def ahead_of(u, dst, dst_top):
        return (*unit(u), dst, dst_top, False)

    def behind_of(u, src, src_top):
        return (*unit(u), src, src_top)

    work(ahead_of(jnp.int32(0), score_a, top_a), None)

    def full(i, _):
        for step, actions in steps.items():
            pl.when(i == step)(do(actions))
        work(ahead_of(2 * i + 1, score_b, top_b), behind_of(2 * i, score_a, top_a))
        work(ahead_of(lax.min(2 * i + 2, UNITS - 1), score_a, top_a), behind_of(2 * i + 1, score_b, top_b))
        return 0

    lax.fori_loop(0, UNITS // 2, full, 0)

    def quarter_of(k):
        return lax.rem(y + k + 1 + jnp.where(k == 0, 1, 0) - jnp.where(k == 1, 1, 0), 4)

    def wide(k):
        p = quarter_of(k)
        return 2 * p + 1 - low, (4 * p + 3 - low, 4 * p + 1 - low)

    def narrow(k):
        p = quarter_of(k)
        return 2 * p + low, (4 * p + low,)

    for where in (wide, narrow):
        work((*where(jnp.int32(0)), score_a, top_a, True), None)

        def edge(k, _, where=where):
            one, two = where(2 * k), where(2 * k + 1)
            work((*two, score_b, top_b, True), (*one, score_a, top_a))
            finish(one[0])
            work((*where(lax.min(2 * k + 2, 3)), score_a, top_a, True), (*two, score_b, top_b))
            finish(two[0])
            return 0

        lax.fori_loop(0, 2, edge, 0)

    for send_sem, index, shape in sent:
        held = {
            (BLOCK, WIDTH): kv.at[0, 0, 0],
            (BLOCK, GROUP): q_in.at[0],
            (2, 2, BLOCK, WIDTH): kv.at[pl.ds(0, 2), 0],
            (2, BLOCK, WIDTH): kv.at[pl.ds(0, 2), 0, 0],
        }[shape]
        pltpu.make_async_remote_copy(
            src_ref=held, dst_ref=held, send_sem=send_sem.at[index], recv_sem=local_sem.at[0], device_id=mate,
            device_id_type=MESH,
        ).wait_send()
    for slot in range(SLOTS):

        @pl.when(slot != my_slot)
        def _():
            done = pltpu.make_async_remote_copy(
                src_ref=o_buf.at[slot],
                dst_ref=out_ref.at[:, pl.ds(slot * GROUP, GROUP)],
                send_sem=out_send.at[slot],
                recv_sem=out_recv.at[slot],
                device_id=mate,
                device_id_type=MESH,
            )
            done.wait_send()
            done.wait_recv()

        @pl.when(slot == my_slot)
        def _():
            pltpu.make_async_copy(o_buf.at[slot], out_ref.at[:, columns(my_head, GROUP)], local_sem.at[0]).wait()


def per_device(queries, keys, values):
    sem = pltpu.SemaphoreType.DMA
    return pl.pallas_call(
        kernel,
        out_shape=jax.ShapeDtypeStruct(queries.shape, BF16),
        in_specs=[pl.BlockSpec(memory_space=pl.ANY)] * 3,
        out_specs=pl.BlockSpec(memory_space=pl.ANY),
        scratch_shapes=[
            pltpu.VMEM((16, 8, 2, BLOCK, WIDTH), BF16),
            pltpu.VMEM((BLOCK, 8 * WIDTH), BF16),
            pltpu.VMEM((8, WIDTH, BLOCK), BF16),
            pltpu.VMEM((SLOTS, BLOCK, GROUP), BF16),
            pltpu.VMEM((SLOTS, ROWS, 2 * WIDTH), BF16),
            pltpu.VMEM((SLOTS, 1, ROWS), F32),
            pltpu.VMEM((SLOTS, 8, ROWS), F32),
            pltpu.VMEM((SLOTS, WIDTH, ROWS), F32),
            pltpu.VMEM((2 * CHUNK, ROWS), F32),
            pltpu.VMEM((2 * CHUNK, ROWS), F32),
            pltpu.VMEM((8, ROWS), F32),
            pltpu.VMEM((8, ROWS), F32),
            pltpu.VMEM((SLOTS, BLOCK, GROUP), BF16),
            sem((4,)),
            sem((3, 7)), sem((3, 8)),
            sem((4,)), sem((4,)),
            sem((4, 2, 2)), sem((4, 2, 2)),
            sem((4, 2, 2)), sem((4, 2, 2)),
            sem((4, 2, 4)), sem((4, 2, 4)),
            sem((8,)), sem((8,)),
        ],
        compiler_params=pltpu.CompilerParams(
            collective_id=0, has_side_effects=True, vmem_limit_bytes=56 * 2**20
        ),
        name="causal_attention",
    )(queries, keys, values)


def solution(mesh):
    spec = P(("ctx", "head"), None)
    return jax.shard_map(per_device, mesh=mesh, in_specs=(spec, spec, spec), out_specs=spec, check_vma=False)
```

```python
import functools

import jax
import jax.numpy as jnp
from jax import lax
from jax.experimental import pallas as pl
from jax.experimental.pallas import tpu as pltpu
from jax.sharding import PartitionSpec as P

BLOCK = 128
WIDTH = 128
GROUP = 4 * WIDTH
ROWS = 4 * BLOCK
CHUNK = 1024
PART = 2048
SPAN = 256
SLOTS = 8
LOG2_SCALE = WIDTH**-0.5 * 1.4426950408889634
MESH = pl.DeviceIdType.MESH
F32 = jnp.float32
BF16 = jnp.bfloat16


def kernel(
    q_ref, k_ref, v_ref, out_ref,
    kv, kv_out, v_raw, q_in, q_pair, peak, total, acc, score_a, score_b, top_a, top_b, o_buf,
    local_sem, load_sem, home_send, home_recv, mate_send, mate_recv, core_send, core_recv, out_send, out_recv,
):
    y = lax.axis_index("ctx")
    head = lax.axis_index("head")
    x, z, c = head // 8, lax.rem(head, 8) // 2, lax.rem(head, 2)
    low_y, low_x, low_z = (lax.min(v, 3 - v) for v in (y, x, z))
    high_y, high_x, high_z = (v // 2 for v in (y, x, z))
    my_slot = my_head = 4 * high_y + 2 * high_x + high_z
    my_chunk, my_row = 4 * high_y + high_x, 4 * c + high_z

    def at(y_, x_, z_, c_):
        return (y_, x_ * 8 + z_ * 2 + c_)

    def beside(v):
        return v + 1 - 2 * lax.rem(v, 2)

    homes = []
    for flip in range(7, 0, -1):
        y_, x_, z_ = (3 - v if flip & bit else v for v, bit in ((y, 4), (x, 2), (z, 1)))
        homes.append((4 * (y_ // 2) + 2 * (x_ // 2) + z_ // 2, at(y_, x_, z_, c)))
    mate_y, mate_x, mate_z = at(beside(y), x, z, c), at(y, beside(x), z, c), at(y, x, beside(z), c)
    twin = at(y, x, z, 1 - c)

    barrier = pltpu.get_barrier_semaphore()
    for other in [to for _, to in homes] + [mate_y, mate_x, mate_z, twin]:
        pl.semaphore_signal(barrier, inc=1, device_id=other, device_id_type=MESH)

    def columns(head_, width):
        return pl.ds(pl.multiple_of(head_ * width, width), width)

    load_v = pltpu.make_async_copy(v_ref, v_raw, local_sem.at[0])
    load_v.start()
    load_k = [
        pltpu.make_async_copy(k_ref.at[:, h * WIDTH : (h + 1) * WIDTH], kv_out.at[h, 0], load_sem.at[h]) for h in range(8)
    ]
    for copy in load_k:
        copy.start()
    own = [pltpu.make_async_copy(q_ref.at[:, columns(my_head, GROUP)], q_in.at[my_slot], local_sem.at[1])]
    own[0].start()
    peak[...] = jnp.full_like(peak, -1e30)
    total[...] = jnp.zeros_like(total)
    acc[...] = jnp.zeros_like(acc)
    load_v.wait()
    for h in range(8):
        kv_out[h, 1] = v_raw[:, h * WIDTH : (h + 1) * WIDTH].T
    for copy in load_k:
        copy.wait()
    own.append(pltpu.make_async_copy(kv_out.at[my_head], kv.at[my_chunk, my_row], local_sem.at[2]))
    own[-1].start()

    pl.semaphore_wait(barrier, 11)

    home, mates, core = (home_send, home_recv), (mate_send, mate_recv), (core_send, core_recv)
    sent = {}

    def send(src, dst, sems, index, device, recv_index=None, noted=None):
        send_sem, recv_sem = sems
        pltpu.make_async_remote_copy(
            src_ref=src,
            dst_ref=dst,
            send_sem=send_sem.at[index],
            recv_sem=recv_sem.at[index if recv_index is None else recv_index],
            device_id=device,
            device_id_type=MESH,
        ).start()
        sent[id(send_sem), noted or index] = (send_sem, src.shape)

    def arrived(dst, recv_sem):
        pltpu.make_async_remote_copy(
            src_ref=dst, dst_ref=dst, send_sem=local_sem.at[0], recv_sem=recv_sem, device_id=twin, device_id_type=MESH
        ).wait_recv()

    def send_kv():
        for i, (there, to) in enumerate(homes):
            send(kv_out.at[there], kv.at[my_chunk, my_row], home, (0, i), to, (0, my_slot))

    pl.when(high_y == 0)(send_kv)
    for i, (there, to) in enumerate(homes):
        send(q_ref.at[:, columns(there, GROUP)], q_in.at[my_slot], home, (1, i), to, (1, my_slot))
    pl.when(high_y == 1)(send_kv)

    for copy in own:
        copy.wait()

    def piece(quarter, chunk, chunks, mz, rows, c_=c):
        return kv.at[pl.ds(4 * quarter + chunk, chunks), pl.ds(4 * c_ + 2 * mz, rows)]

    def block(quarter, chunk, row, c_=c):
        return kv.at[4 * quarter + chunk, 4 * c_ + row]

    def pass_on(src, dst, quarter, number, device):
        send(src, dst, mates, (quarter, number), device)

    def to_twin(quarter, number, *what):
        send(piece(quarter, *what), piece(quarter, *what), core, (quarter, number), twin)

    def got(quarter, number, *what):
        arrived(piece(quarter, *what), mate_recv.at[quarter, number])

    def of_twin(quarter, number, *what):
        arrived(piece(quarter, *what, 1 - c), core_recv.at[quarter, number])

    def own_1(q):
        for i, (dx, dz) in enumerate(((0, 0), (0, 1), (1, 0), (1, 1))):
            hx, hz = lax.rem(high_x + dx, 2), lax.rem(high_z + dz, 2)
            this, there, slot = block(q, hx, hz), 2 * hx + hz, 4 * q + 2 * hx + hz

            @pl.when(slot != my_slot)
            def _():
                arrived(this, home_recv.at[0, slot])

            send(this, block(q, hx, 2 + hz), mates, (q, 4 + there), mate_z, noted=(q, 4 + i))
            send(this, block(q, 2 + hx, hz), mates, (q, there), mate_x, noted=(q, i))
            send(this, this, core, (q, there), twin, noted=(q, i))
            send(this, block(2 + q, hx, hz), mates, (2 + q, there), mate_y, noted=(2 + q, i))

    def own_2(q):
        for i in range(4):
            arrived(block(q, i // 2, 2 + i % 2), mate_recv.at[q, 4 + i])
        to_twin(q, 4, 0, 2, 1, 2)
        pass_on(piece(q, 1, 1, 1, 2), piece(q, 3, 1, 1, 2), q, 8, mate_x)
        pass_on(piece(q, 1, 1, 1, 2), piece(2 + q, 1, 1, 1, 2), 2 + q, 4, mate_y)

    def own_3(q):
        for i in range(4):
            arrived(block(q, 2 + i // 2, i % 2), mate_recv.at[q, i])
        pass_on(piece(q, 2, 1, 0, 2), piece(q, 2, 1, 1, 2), q, 9, mate_z)
        to_twin(q, 5, 2, 2, 0, 2)
        pass_on(piece(q, 2, 1, 0, 2), piece(2 + q, 2, 1, 0, 2), 2 + q, 5, mate_y)

    def own_4(q):
        got(q, 8, 3, 1, 1, 2)
        got(q, 9, 2, 1, 1, 2)
        to_twin(q, 6, 2, 2, 1, 2)

    def own_twin_1(q):
        for i in range(4):
            arrived(block(q, i // 2, i % 2, 1 - c), core_recv.at[q, i])
        of_twin(q, 4, 0, 2, 1, 2)

    def own_twin_2(q):
        of_twin(q, 5, 2, 2, 0, 2)
        of_twin(q, 6, 2, 2, 1, 2)

    def mate_1(q):
        q = 2 + q
        for i in range(4):
            arrived(block(q, i // 2, i % 2), mate_recv.at[q, i])
        pass_on(piece(q, 0, 1, 0, 2), piece(q, 0, 1, 1, 2), q, 6, mate_z)
        pass_on(piece(q, 1, 1, 0, 2), piece(q, 3, 1, 0, 2), q, 7, mate_x)
        to_twin(q, 0, 0, 2, 0, 2)

    def mate_2(q):
        q = 2 + q
        got(q, 5, 2, 1, 0, 2)
        pass_on(piece(q, 2, 1, 0, 2), piece(q, 2, 1, 1, 2), q, 8, mate_z)
        to_twin(q, 1, 2, 1, 0, 2)
        got(q, 4, 1, 1, 1, 2)
        pass_on(piece(q, 1, 1, 1, 2), piece(q, 3, 1, 1, 2), q, 9, mate_x)
        to_twin(q, 2, 1, 1, 1, 2)

    def mate_3(q):
        q = 2 + q
        got(q, 6, 0, 1, 1, 2)
        to_twin(q, 3, 0, 1, 1, 2)

    def mate_4(q):
        q = 2 + q
        got(q, 7, 3, 1, 0, 2)
        to_twin(q, 4, 3, 1, 0, 2)
        got(q, 8, 2, 1, 1, 2)
        to_twin(q, 5, 2, 1, 1, 2)
        got(q, 9, 3, 1, 1, 2)
        to_twin(q, 6, 3, 1, 1, 2)

    def mate_twin_1(q):
        q = 2 + q
        of_twin(q, 0, 0, 2, 0, 2)
        of_twin(q, 2, 1, 1, 1, 2)
        of_twin(q, 3, 0, 1, 1, 2)

    def mate_twin_2(q):
        q = 2 + q
        for number, (chunk, mz) in ((1, (2, 0)), (4, (3, 0)), (5, (2, 1)), (6, (3, 1))):
            of_twin(q, number, chunk, 1, mz, 2)

    def split_queries(slot):
        @pl.when(slot != my_slot)
        def _():
            arrived(q_in.at[slot], home_recv.at[1, slot])

        for h in range(4):
            scaled = q_in[slot, :, h * WIDTH : (h + 1) * WIDTH].astype(F32) * LOG2_SCALE
            first = scaled.astype(BF16)
            q_pair[slot, h * BLOCK : (h + 1) * BLOCK, :WIDTH] = first
            q_pair[slot, h * BLOCK : (h + 1) * BLOCK, WIDTH:] = (scaled - first.astype(F32)).astype(BF16)

    order = []
    for z_ in range(4):
        mz = low_z if min(z_, 3 - z_) == 0 else 1 - low_z
        order += [4 * c_ + 2 * mz + z_ // 2 for c_ in range(2)]

    def parts(chunks):
        blocks = [(chunk, row) for chunk in chunks for row in order]
        return [blocks[i : i + PART // BLOCK] for i in range(0, len(blocks), PART // BLOCK)]

    def work(ahead, behind):
        ahead_parts = parts(ahead[1]) if ahead else []
        behind_parts = parts(behind[1]) if behind else []
        for start in range(0, ROWS, SPAN):
            columns_ = slice(start, start + SPAN)
            if behind:
                slot, _, src, src_top = behind
                old = peak[slot, :, columns_]
                new = jnp.maximum(old, jnp.max(src_top[:, columns_], axis=0, keepdims=True))
                rescale = jnp.exp2(old - new)
                peak[slot, :, columns_] = new
                sums, mixture = total[slot, :, columns_] * rescale, None
            highest = None
            for i in range(max(len(ahead_parts), len(behind_parts))):
                if i < len(ahead_parts):
                    slot_, chunks_, dst, dst_top, offset = ahead
                    k = jnp.concatenate([kv[chunk, b, 0] for chunk, b in ahead_parts[i]], axis=0)
                    rows = slice(i * PART, i * PART + k.shape[0])
                    s = lax.dot_general(
                        jnp.concatenate([k, k], axis=1), q_pair[slot_, columns_], (((1,), (1,)), ((), ())),
                        preferred_element_type=F32,
                    )
                    if offset is not None and rows.stop > CHUNK * (len(chunks_) - 1):
                        past = rows.start - CHUNK * (len(chunks_) - 1)
                        key = past + lax.broadcasted_iota(jnp.int32, s.shape, 0)
                        token = lax.rem(lax.broadcasted_iota(jnp.int32, s.shape, 1), BLOCK)
                        s = jnp.where(key <= token + offset, s, -1e30)
                    dst[rows, columns_] = s
                    best = jnp.max(s.reshape(-1, 8, SPAN), axis=0)
                    highest = best if highest is None else jnp.maximum(highest, best)
                if i < len(behind_parts):
                    rows = slice(i * PART, i * PART + BLOCK * len(behind_parts[i]))
                    weights = jnp.exp2(src[rows, columns_] - new)
                    sums = sums + jnp.sum(weights.reshape(-1, 8, SPAN), axis=0)
                    v = jnp.concatenate([kv[chunk, b, 1] for chunk, b in behind_parts[i]], axis=1)
                    term = jnp.dot(v, weights.astype(BF16), preferred_element_type=F32)
                    mixture = term if mixture is None else mixture + term
            if ahead:
                dst_top[:, columns_] = highest
            if behind:
                total[slot, :, columns_] = sums
                acc[slot, :, columns_] = acc[slot, :, columns_] * rescale + mixture

    def finish(slot):
        for h in range(4):
            columns_ = slice(h * BLOCK, (h + 1) * BLOCK)
            part = acc[slot, :, columns_] / jnp.sum(total[slot, :, columns_], axis=0, keepdims=True)
            o_buf[slot, :, h * WIDTH : (h + 1) * WIDTH] = part.T.astype(BF16)

        @pl.when(slot != my_slot)
        def _():
            pltpu.make_async_remote_copy(
                src_ref=o_buf.at[slot],
                dst_ref=out_ref.at[:, columns(my_head, GROUP)],
                send_sem=out_send.at[slot],
                recv_sem=out_recv.at[my_head],
                device_id=at(
                    low_y + slot // 4 * (3 - 2 * low_y),
                    low_x + lax.rem(slot, 4) // 2 * (3 - 2 * low_x),
                    low_z + lax.rem(slot, 2) * (3 - 2 * low_z),
                    c,
                ),
                device_id_type=MESH,
            ).start()

        @pl.when(slot == my_slot)
        def _():
            pltpu.make_async_copy(o_buf.at[slot], out_ref.at[:, columns(my_head, GROUP)], local_sem.at[0]).start()

    def lower_queries(_):
        for slot in range(4):
            split_queries(slot)

    own_1(0)
    own_2(0)
    own_3(0)
    for slot in range(4, 8):
        split_queries(slot)
    own_twin_1(0)

    def side_of(k):
        return lax.rem(high_z + 3 - k, 2)

    def lead_edge(r, k):
        return 4 * r + 2 + side_of(k), (4 * r, 4 * r + 2)

    def wide_edge(r, k):
        return 4 * r + 2 * (1 - low_x) + side_of(k), (4 * r + 3 - low_x, 4 * r + 1 - low_x)

    def narrow_edge(r, k):
        return 4 * r + 2 * low_x + side_of(k), (4 * r + low_x,)

    def offset_of(k):
        return BLOCK * (2 * (low_z + side_of(k) * (3 - 2 * low_z)) + c)

    def among(r, k, m):
        upper, quarter = 1 - (1 - r) * low_y, 2 + r * (1 - low_y)
        hx = low_x if m < 2 else 1 - low_x
        chunk = 4 * quarter + 2 * (m % 2)
        return 4 * upper + 2 * hx + side_of(k), (chunk, chunk + 1)

    def pick(first, one, other):
        (slot, (a_, b_)), (slot_, (c_, d_)) = one, other
        return jnp.where(first, slot, slot_), (jnp.where(first, a_, c_), jnp.where(first, b_, d_))

    def unit(r, j):
        past = j - (8 - 8 * r)
        first = 2 * (lax.rem(j, 8) // 4)
        later = pick(past < 2, lead_edge(r, past), among(r, 0, 0))
        return pick(past < 0, (4 + lax.rem(j, 4), (first, first + 1)), later)

    steps = {
        0: [(own_4, 0), (mate_1, 0)],
        1: [(own_twin_2, 0), (mate_2, 0)],
        2: [(own_1, 1)],
        3: [(mate_3, 0), (mate_4, 0), (lower_queries, 0)],
        4: [(mate_twin_1, 0), (own_2, 1), (own_3, 1)],
        5: [(mate_4, 1), (mate_twin_1, 1)],
    }
    places = {
        (0, 0, 0): [(mate_twin_2, 0), (mate_1, 1)],
        (0, 0, 1): [(mate_2, 1), (own_4, 1)],
        (0, 1, 1): [(own_twin_1, 1), (own_twin_2, 1), (mate_3, 1)],
        (1, 0, 0): [(mate_twin_2, 1)],
    }

    def do(actions):
        def run():
            for action, quarter in actions:
                action(quarter)

        return run

    a, b = (score_a, top_a), (score_b, top_b)
    zero = jnp.int32(0)
    work((*unit(zero, zero), *a, None), None)

    def full(r, i, _):
        for step, actions in steps.items():
            pl.when(i + 5 * r == step)(do(actions))
        work((*unit(r, 2 * i + 1), *b, None), (*unit(r, 2 * i), *a))
        work((*unit(r, 2 * i + 2), *a, None), (*unit(r, 2 * i + 1), *b))
        return 0

    def slots(r, k, _):
        def at_place(number):
            for (r_, k_, number_), actions in places.items():
                if number_ == number:
                    pl.when((r == r_) & (k == k_))(do(actions))

        offset = offset_of(k)
        wide, narrow = wide_edge(r, k), narrow_edge(r, k)
        after = pick(k == 0, among(r, 1, 0), lead_edge(1, 0))
        at_place(0)
        work((*among(r, k, 1), *b, None), (*among(r, k, 0), *a))
        work((*narrow, *a, offset), (*among(r, k, 1), *b))
        work((*among(r, k, 2), *b, None), (*narrow, *a))
        finish(narrow[0])
        at_place(1)
        work((*among(r, k, 3), *a, None), (*among(r, k, 2), *b))
        work((*wide, *b, offset), (*among(r, k, 3), *a))
        work((*after, *a, None), (*wide, *b))
        finish(wide[0])
        return 0

    def round_(r, _):
        lax.fori_loop(0, 5 - 4 * r, functools.partial(full, r), 0)
        lax.fori_loop(0, 2, functools.partial(slots, r), 0)
        return 0

    lax.fori_loop(0, 2, round_, 0)

    for (_, index), (send_sem, shape) in sent.items():
        held = {
            (BLOCK, GROUP): q_in.at[0],
            (2, BLOCK, WIDTH): kv.at[0, 0],
            (1, 2, 2, BLOCK, WIDTH): kv.at[pl.ds(0, 1), pl.ds(0, 2)],
            (2, 2, 2, BLOCK, WIDTH): kv.at[pl.ds(0, 2), pl.ds(0, 2)],
        }[shape]
        pltpu.make_async_remote_copy(
            src_ref=held, dst_ref=held, send_sem=send_sem.at[index], recv_sem=local_sem.at[0], device_id=twin,
            device_id_type=MESH,
        ).wait_send()
    for slot in range(SLOTS):

        @pl.when(slot != my_slot)
        def _():
            done = pltpu.make_async_remote_copy(
                src_ref=o_buf.at[slot],
                dst_ref=out_ref.at[:, pl.ds(slot * GROUP, GROUP)],
                send_sem=out_send.at[slot],
                recv_sem=out_recv.at[slot],
                device_id=twin,
                device_id_type=MESH,
            )
            done.wait_send()
            done.wait_recv()

        @pl.when(slot == my_slot)
        def _():
            pltpu.make_async_copy(o_buf.at[slot], out_ref.at[:, columns(my_head, GROUP)], local_sem.at[0]).wait()


def per_device(queries, keys, values):
    sem = pltpu.SemaphoreType.DMA
    return pl.pallas_call(
        kernel,
        out_shape=jax.ShapeDtypeStruct(queries.shape, BF16),
        in_specs=[pl.BlockSpec(memory_space=pl.ANY)] * 3,
        out_specs=pl.BlockSpec(memory_space=pl.ANY),
        scratch_shapes=[
            pltpu.VMEM((16, 8, 2, BLOCK, WIDTH), BF16),
            pltpu.VMEM((8, 2, BLOCK, WIDTH), BF16),
            pltpu.VMEM((BLOCK, 8 * WIDTH), BF16),
            pltpu.VMEM((SLOTS, BLOCK, GROUP), BF16),
            pltpu.VMEM((SLOTS, ROWS, 2 * WIDTH), BF16),
            pltpu.VMEM((SLOTS, 1, ROWS), F32),
            pltpu.VMEM((SLOTS, 8, ROWS), F32),
            pltpu.VMEM((SLOTS, WIDTH, ROWS), F32),
            pltpu.VMEM((2 * CHUNK, ROWS), F32),
            pltpu.VMEM((2 * CHUNK, ROWS), F32),
            pltpu.VMEM((8, ROWS), F32),
            pltpu.VMEM((8, ROWS), F32),
            pltpu.VMEM((SLOTS, BLOCK, GROUP), BF16),
            sem((4,)), sem((8,)),
            sem((2, 7)), sem((2, 8)),
            sem((4, 10)), sem((4, 10)),
            sem((4, 7)), sem((4, 7)),
            sem((8,)), sem((8,)),
        ],
        compiler_params=pltpu.CompilerParams(
            collective_id=0, has_side_effects=True, vmem_limit_bytes=56 * 2**20
        ),
        name="causal_attention",
    )(queries, keys, values)


def solution(mesh):
    spec = P(("ctx", "head"), None)
    return jax.shard_map(per_device, mesh=mesh, in_specs=(spec, spec, spec), out_specs=spec, check_vma=False)
```

```python
import functools

import jax
import jax.numpy as jnp
from jax import lax
from jax.experimental import pallas as pl
from jax.experimental.pallas import tpu as pltpu
from jax.sharding import PartitionSpec as P

BLOCK = 128
WIDTH = 128
GROUP = 4 * WIDTH
ROWS = 4 * BLOCK
CHUNK = 1024
PART = 2048
SPAN = 256
SLOTS = 8
LOG2_SCALE = WIDTH**-0.5 * 1.4426950408889634
MESH = pl.DeviceIdType.MESH
F32 = jnp.float32
BF16 = jnp.bfloat16


def kernel(
    q_ref, k_ref, v_ref, out_ref,
    kv, kv_out, v_raw, q_in, q_pair, peak, total, acc, score_a, score_b, top_a, top_b, o_buf,
    local_sem, load_sem, home_send, home_recv, mate_send, mate_recv, core_send, core_recv, out_send, out_recv,
):
    y = lax.axis_index("ctx")
    head = lax.axis_index("head")
    x, z, c = head // 8, lax.rem(head, 8) // 2, lax.rem(head, 2)
    low_y, low_x, low_z = (lax.min(v, 3 - v) for v in (y, x, z))
    high_y, high_x, high_z = (v // 2 for v in (y, x, z))
    my_slot = my_head = 4 * high_y + 2 * high_x + high_z
    my_chunk, my_row = 4 * high_y + high_x, 4 * c + high_z

    def at(y_, x_, z_, c_):
        return (y_, x_ * 8 + z_ * 2 + c_)

    def beside(v):
        return v + 1 - 2 * lax.rem(v, 2)

    homes = []
    for flip in range(7, 0, -1):
        y_, x_, z_ = (3 - v if flip & bit else v for v, bit in ((y, 4), (x, 2), (z, 1)))
        homes.append((4 * (y_ // 2) + 2 * (x_ // 2) + z_ // 2, at(y_, x_, z_, c)))
    mate_y, mate_x, mate_z = at(beside(y), x, z, c), at(y, beside(x), z, c), at(y, x, beside(z), c)
    twin = at(y, x, z, 1 - c)

    barrier = pltpu.get_barrier_semaphore()
    for other in [to for _, to in homes] + [mate_y, mate_x, mate_z, twin]:
        pl.semaphore_signal(barrier, inc=1, device_id=other, device_id_type=MESH)

    def columns(head_, width):
        return pl.ds(pl.multiple_of(head_ * width, width), width)

    load_v = pltpu.make_async_copy(v_ref, v_raw, local_sem.at[0])
    load_v.start()
    load_k = [
        pltpu.make_async_copy(k_ref.at[:, h * WIDTH : (h + 1) * WIDTH], kv_out.at[h, 0], load_sem.at[h]) for h in range(8)
    ]
    for copy in load_k:
        copy.start()
    own = [pltpu.make_async_copy(q_ref.at[:, columns(my_head, GROUP)], q_in.at[my_slot], local_sem.at[1])]
    own[0].start()
    peak[...] = jnp.full_like(peak, -1e30)
    total[...] = jnp.zeros_like(total)
    acc[...] = jnp.zeros_like(acc)
    pl.semaphore_wait(barrier, 11)

    home, mates, core = (home_send, home_recv), (mate_send, mate_recv), (core_send, core_recv)
    sent = {}

    def send(src, dst, sems, index, device, recv_index=None, noted=None):
        send_sem, recv_sem = sems
        pltpu.make_async_remote_copy(
            src_ref=src,
            dst_ref=dst,
            send_sem=send_sem.at[index],
            recv_sem=recv_sem.at[index if recv_index is None else recv_index],
            device_id=device,
            device_id_type=MESH,
        ).start()
        sent[id(send_sem), noted or index] = (send_sem, src.shape)

    def arrived(dst, recv_sem):
        pltpu.make_async_remote_copy(
            src_ref=dst, dst_ref=dst, send_sem=local_sem.at[0], recv_sem=recv_sem, device_id=twin, device_id_type=MESH
        ).wait_recv()

    def send_queries():
        for i, (there, to) in enumerate(homes):
            send(q_ref.at[:, columns(there, GROUP)], q_in.at[my_slot], home, (1, i), to, (1, my_slot))

    def send_kv():
        for i, (there, to) in enumerate(homes):
            send(kv_out.at[there], kv.at[my_chunk, my_row], home, (0, i), to, (0, my_slot))

    pl.when(high_y == 1)(send_queries)
    load_v.wait()
    for h in range(8):
        kv_out[h, 1] = v_raw[:, h * WIDTH : (h + 1) * WIDTH].T
    for copy in load_k:
        copy.wait()
    pl.when(high_y == 0)(send_kv)
    own.append(pltpu.make_async_copy(kv_out.at[my_head], kv.at[my_chunk, my_row], local_sem.at[2]))
    own[-1].start()
    for copy in own:
        copy.wait()

    def piece(quarter, chunk, chunks, mz, rows, c_=c):
        return kv.at[pl.ds(4 * quarter + chunk, chunks), pl.ds(4 * c_ + 2 * mz, rows)]

    def block(quarter, chunk, row, c_=c):
        return kv.at[4 * quarter + chunk, 4 * c_ + row]

    def pass_on(src, dst, quarter, number, device):
        send(src, dst, mates, (quarter, number), device)

    def to_twin(quarter, number, *what):
        send(piece(quarter, *what), piece(quarter, *what), core, (quarter, number), twin)

    def got(quarter, number, *what):
        arrived(piece(quarter, *what), mate_recv.at[quarter, number])

    def of_twin(quarter, number, *what):
        arrived(piece(quarter, *what, 1 - c), core_recv.at[quarter, number])

    def own_1(q):
        for i, (dx, dz) in enumerate(((0, 0), (0, 1), (1, 0), (1, 1))):
            hx, hz = lax.rem(high_x + dx, 2), lax.rem(high_z + dz, 2)
            this, there, slot = block(q, hx, hz), 2 * hx + hz, 4 * q + 2 * hx + hz

            @pl.when(slot != my_slot)
            def _():
                arrived(this, home_recv.at[0, slot])

            send(this, block(q, hx, 2 + hz), mates, (q, 4 + there), mate_z, noted=(q, 4 + i))
            send(this, block(q, 2 + hx, hz), mates, (q, there), mate_x, noted=(q, i))
            send(this, this, core, (q, there), twin, noted=(q, i))
            send(this, block(2 + q, hx, hz), mates, (2 + q, there), mate_y, noted=(2 + q, i))

    def own_2(q):
        for i in range(4):
            arrived(block(q, i // 2, 2 + i % 2), mate_recv.at[q, 4 + i])
        to_twin(q, 4, 0, 2, 1, 2)
        pass_on(piece(q, 1, 1, 1, 2), piece(q, 3, 1, 1, 2), q, 8, mate_x)
        pass_on(piece(q, 1, 1, 1, 2), piece(2 + q, 1, 1, 1, 2), 2 + q, 4, mate_y)

    def own_3(q):
        for i in range(4):
            arrived(block(q, 2 + i // 2, i % 2), mate_recv.at[q, i])
        pass_on(piece(q, 2, 1, 0, 2), piece(q, 2, 1, 1, 2), q, 9, mate_z)
        to_twin(q, 5, 2, 2, 0, 2)
        pass_on(piece(q, 2, 1, 0, 2), piece(2 + q, 2, 1, 0, 2), 2 + q, 5, mate_y)

    def own_4(q):
        got(q, 8, 3, 1, 1, 2)
        got(q, 9, 2, 1, 1, 2)
        to_twin(q, 6, 2, 2, 1, 2)

    def own_twin_1(q):
        for i in range(4):
            arrived(block(q, i // 2, i % 2, 1 - c), core_recv.at[q, i])
        of_twin(q, 4, 0, 2, 1, 2)

    def own_twin_2(q):
        of_twin(q, 5, 2, 2, 0, 2)
        of_twin(q, 6, 2, 2, 1, 2)

    def mate_1(q):
        q = 2 + q
        for i in range(4):
            arrived(block(q, i // 2, i % 2), mate_recv.at[q, i])
        pass_on(piece(q, 0, 1, 0, 2), piece(q, 0, 1, 1, 2), q, 6, mate_z)
        pass_on(piece(q, 1, 1, 0, 2), piece(q, 3, 1, 0, 2), q, 7, mate_x)
        to_twin(q, 0, 0, 2, 0, 2)

    def mate_2(q):
        q = 2 + q
        got(q, 5, 2, 1, 0, 2)
        pass_on(piece(q, 2, 1, 0, 2), piece(q, 2, 1, 1, 2), q, 8, mate_z)
        to_twin(q, 1, 2, 1, 0, 2)
        got(q, 4, 1, 1, 1, 2)
        pass_on(piece(q, 1, 1, 1, 2), piece(q, 3, 1, 1, 2), q, 9, mate_x)
        to_twin(q, 2, 1, 1, 1, 2)

    def mate_3(q):
        q = 2 + q
        got(q, 6, 0, 1, 1, 2)
        to_twin(q, 3, 0, 1, 1, 2)

    def mate_4(q):
        q = 2 + q
        got(q, 7, 3, 1, 0, 2)
        to_twin(q, 4, 3, 1, 0, 2)
        got(q, 8, 2, 1, 1, 2)
        to_twin(q, 5, 2, 1, 1, 2)
        got(q, 9, 3, 1, 1, 2)
        to_twin(q, 6, 3, 1, 1, 2)

    def mate_twin_1(q):
        q = 2 + q
        of_twin(q, 0, 0, 2, 0, 2)
        of_twin(q, 2, 1, 1, 1, 2)
        of_twin(q, 3, 0, 1, 1, 2)

    def mate_twin_2(q):
        q = 2 + q
        for number, (chunk, mz) in ((1, (2, 0)), (4, (3, 0)), (5, (2, 1)), (6, (3, 1))):
            of_twin(q, number, chunk, 1, mz, 2)

    def split_queries(slot):
        @pl.when(slot != my_slot)
        def _():
            arrived(q_in.at[slot], home_recv.at[1, slot])

        for h in range(4):
            scaled = q_in[slot, :, h * WIDTH : (h + 1) * WIDTH].astype(F32) * LOG2_SCALE
            first = scaled.astype(BF16)
            q_pair[slot, h * BLOCK : (h + 1) * BLOCK, :WIDTH] = first
            q_pair[slot, h * BLOCK : (h + 1) * BLOCK, WIDTH:] = (scaled - first.astype(F32)).astype(BF16)

    order = []
    for z_ in range(4):
        mz = low_z if min(z_, 3 - z_) == 0 else 1 - low_z
        order += [4 * c_ + 2 * mz + z_ // 2 for c_ in range(2)]

    def parts(chunks):
        blocks = [(chunk, row) for chunk in chunks for row in order]
        return [blocks[i : i + PART // BLOCK] for i in range(0, len(blocks), PART // BLOCK)]

    def work(ahead, behind):
        ahead_parts = parts(ahead[1]) if ahead else []
        behind_parts = parts(behind[1]) if behind else []
        for start in range(0, ROWS, SPAN):
            columns_ = slice(start, start + SPAN)
            if behind:
                slot, _, src, src_top = behind
                old = peak[slot, :, columns_]
                new = jnp.maximum(old, jnp.max(src_top[:, columns_], axis=0, keepdims=True))
                rescale = jnp.exp2(old - new)
                peak[slot, :, columns_] = new
                sums, mixture = total[slot, :, columns_] * rescale, None
            highest = None
            for i in range(max(len(ahead_parts), len(behind_parts))):
                if i < len(ahead_parts):
                    slot_, chunks_, dst, dst_top, offset = ahead
                    k = jnp.concatenate([kv[chunk, b, 0] for chunk, b in ahead_parts[i]], axis=0)
                    rows = slice(i * PART, i * PART + k.shape[0])
                    s = lax.dot_general(
                        jnp.concatenate([k, k], axis=1), q_pair[slot_, columns_], (((1,), (1,)), ((), ())),
                        preferred_element_type=F32,
                    )
                    if offset is not None and rows.stop > CHUNK * (len(chunks_) - 1):
                        past = rows.start - CHUNK * (len(chunks_) - 1)
                        key = past + lax.broadcasted_iota(jnp.int32, s.shape, 0)
                        token = lax.rem(lax.broadcasted_iota(jnp.int32, s.shape, 1), BLOCK)
                        s = jnp.where(key <= token + offset, s, -1e30)
                    dst[rows, columns_] = s
                    best = jnp.max(s.reshape(-1, 8, SPAN), axis=0)
                    highest = best if highest is None else jnp.maximum(highest, best)
                if i < len(behind_parts):
                    rows = slice(i * PART, i * PART + BLOCK * len(behind_parts[i]))
                    weights = jnp.exp2(src[rows, columns_] - new)
                    sums = sums + jnp.sum(weights.reshape(-1, 8, SPAN), axis=0)
                    v = jnp.concatenate([kv[chunk, b, 1] for chunk, b in behind_parts[i]], axis=1)
                    term = jnp.dot(v, weights.astype(BF16), preferred_element_type=F32)
                    mixture = term if mixture is None else mixture + term
            if ahead:
                dst_top[:, columns_] = highest
            if behind:
                total[slot, :, columns_] = sums
                acc[slot, :, columns_] = acc[slot, :, columns_] * rescale + mixture

    def finish(slot):
        for h in range(4):
            columns_ = slice(h * BLOCK, (h + 1) * BLOCK)
            part = acc[slot, :, columns_] / jnp.sum(total[slot, :, columns_], axis=0, keepdims=True)
            o_buf[slot, :, h * WIDTH : (h + 1) * WIDTH] = part.T.astype(BF16)

        @pl.when(slot != my_slot)
        def _():
            pltpu.make_async_remote_copy(
                src_ref=o_buf.at[slot],
                dst_ref=out_ref.at[:, columns(my_head, GROUP)],
                send_sem=out_send.at[slot],
                recv_sem=out_recv.at[my_head],
                device_id=at(
                    low_y + slot // 4 * (3 - 2 * low_y),
                    low_x + lax.rem(slot, 4) // 2 * (3 - 2 * low_x),
                    low_z + lax.rem(slot, 2) * (3 - 2 * low_z),
                    c,
                ),
                device_id_type=MESH,
            ).start()

        @pl.when(slot == my_slot)
        def _():
            pltpu.make_async_copy(o_buf.at[slot], out_ref.at[:, columns(my_head, GROUP)], local_sem.at[0]).start()

    def lower_queries(_):
        for slot in range(4):
            split_queries(slot)

    own_1(0)
    pl.when(high_y == 0)(send_queries)
    own_2(0)
    own_3(0)
    pl.when(high_y == 1)(send_kv)
    for slot in range(4, 8):
        split_queries(slot)
    own_twin_1(0)

    def side_of(k):
        return lax.rem(high_z + 3 - k, 2)

    def lead_edge(r, k):
        return 4 * r + 2 + side_of(k), (4 * r, 4 * r + 2)

    def wide_edge(r, k):
        return 4 * r + 2 * (1 - low_x) + side_of(k), (4 * r + 3 - low_x, 4 * r + 1 - low_x)

    def narrow_edge(r, k):
        return 4 * r + 2 * low_x + side_of(k), (4 * r + low_x,)

    def offset_of(k):
        return BLOCK * (2 * (low_z + side_of(k) * (3 - 2 * low_z)) + c)

    narrow_last = lax.rem(high_x + low_x + 1, 2)

    def among(r, k, m):
        upper, quarter = 1 - (1 - r) * low_y, 2 + r * (1 - low_y)
        hx = 1 - high_x if m < 2 else high_x
        chunk = 4 * quarter + 2 * (m % 2)
        return 4 * upper + 2 * hx + side_of(k), (chunk, chunk + 1)

    def pick(first, one, other):
        (slot, (a_, b_)), (slot_, (c_, d_)) = one, other
        return jnp.where(first, slot, slot_), (jnp.where(first, a_, c_), jnp.where(first, b_, d_))

    def unit(r, j):
        past = j - (8 - 8 * r)
        first = 2 * (lax.rem(j, 8) // 4)
        later = pick(past < 2, lead_edge(r, past), among(r, 0, 0))
        return pick(past < 0, (4 + lax.rem(j, 4), (first, first + 1)), later)

    steps = {
        0: [(mate_1, 0)],
        1: [(own_4, 0), (mate_2, 0)],
        2: [(own_1, 1)],
        3: [(mate_3, 0), (mate_4, 0), (lower_queries, 0)],
        4: [(mate_twin_1, 0)],
        5: [(mate_4, 1), (mate_twin_1, 1)],
    }
    places = {
        (0, 0, 0): [(mate_twin_2, 0), (own_2, 1), (own_3, 1)],
        (0, 0, 1): [(mate_1, 1), (own_4, 1)],
        (0, 1, 0): [(mate_2, 1)],
        (0, 1, 1): [(own_twin_1, 1), (own_twin_2, 1), (mate_3, 1)],
        (1, 0, 0): [(mate_twin_2, 1)],
    }

    def do(actions):
        def run():
            for action, quarter in actions:
                action(quarter)

        return run

    a, b = (score_a, top_a), (score_b, top_b)
    zero = jnp.int32(0)
    work((*unit(zero, zero), *a, None), None)

    def full(r, i, _):
        for step, actions in steps.items():
            pl.when(i + 5 * r == step)(do(actions))
        work((*unit(r, 2 * i + 1), *b, None), (*unit(r, 2 * i), *a))
        pl.when(i + 5 * r == 1)(do([(own_twin_2, 0)]))
        work((*unit(r, 2 * i + 2), *a, None), (*unit(r, 2 * i + 1), *b))
        return 0

    def slots(r, k, _):
        def at_place(number):
            for (r_, k_, number_), actions in places.items():
                if number_ == number:
                    pl.when((r == r_) & (k == k_))(do(actions))

        offset = offset_of(k)
        edges = narrow_edge(r, k), wide_edge(r, k)
        after = pick(k == 0, among(r, 1, 0), lead_edge(1, 0))

        def visit(one, two):
            at_place(0)
            work((*among(r, k, 1), *b, None), (*among(r, k, 0), *a))
            work((*one, *a, offset), (*among(r, k, 1), *b))
            work((*among(r, k, 2), *b, None), (*one, *a))
            finish(one[0])
            at_place(1)
            work((*among(r, k, 3), *a, None), (*among(r, k, 2), *b))
            work((*two, *b, offset), (*among(r, k, 3), *a))
            work((*after, *a, None), (*two, *b))
            finish(two[0])

        pl.when(narrow_last == 0)(lambda: visit(*edges))
        pl.when(narrow_last == 1)(lambda: visit(*edges[::-1]))
        return 0

    def round_(r, _):
        lax.fori_loop(0, 5 - 4 * r, functools.partial(full, r), 0)
        lax.fori_loop(0, 2, functools.partial(slots, r), 0)
        return 0

    lax.fori_loop(0, 2, round_, 0)

    for (_, index), (send_sem, shape) in sent.items():
        held = {
            (BLOCK, GROUP): q_in.at[0],
            (2, BLOCK, WIDTH): kv.at[0, 0],
            (1, 2, 2, BLOCK, WIDTH): kv.at[pl.ds(0, 1), pl.ds(0, 2)],
            (2, 2, 2, BLOCK, WIDTH): kv.at[pl.ds(0, 2), pl.ds(0, 2)],
        }[shape]
        pltpu.make_async_remote_copy(
            src_ref=held, dst_ref=held, send_sem=send_sem.at[index], recv_sem=local_sem.at[0], device_id=twin,
            device_id_type=MESH,
        ).wait_send()
    for slot in range(SLOTS):

        @pl.when(slot != my_slot)
        def _():
            done = pltpu.make_async_remote_copy(
                src_ref=o_buf.at[slot],
                dst_ref=out_ref.at[:, pl.ds(slot * GROUP, GROUP)],
                send_sem=out_send.at[slot],
                recv_sem=out_recv.at[slot],
                device_id=twin,
                device_id_type=MESH,
            )
            done.wait_send()
            done.wait_recv()

        @pl.when(slot == my_slot)
        def _():
            pltpu.make_async_copy(o_buf.at[slot], out_ref.at[:, columns(my_head, GROUP)], local_sem.at[0]).wait()


def per_device(queries, keys, values):
    sem = pltpu.SemaphoreType.DMA
    return pl.pallas_call(
        kernel,
        out_shape=pltpu.VMEM(queries.shape, BF16),
        in_specs=[pl.BlockSpec(memory_space=pl.ANY)] * 3,
        out_specs=pl.BlockSpec(memory_space=pltpu.VMEM),
        scratch_shapes=[
            pltpu.VMEM((16, 8, 2, BLOCK, WIDTH), BF16),
            pltpu.VMEM((8, 2, BLOCK, WIDTH), BF16),
            pltpu.VMEM((BLOCK, 8 * WIDTH), BF16),
            pltpu.VMEM((SLOTS, BLOCK, GROUP), BF16),
            pltpu.VMEM((SLOTS, ROWS, 2 * WIDTH), BF16),
            pltpu.VMEM((SLOTS, 1, ROWS), F32),
            pltpu.VMEM((SLOTS, 8, ROWS), F32),
            pltpu.VMEM((SLOTS, WIDTH, ROWS), F32),
            pltpu.VMEM((2 * CHUNK, ROWS), F32),
            pltpu.VMEM((2 * CHUNK, ROWS), F32),
            pltpu.VMEM((8, ROWS), F32),
            pltpu.VMEM((8, ROWS), F32),
            pltpu.VMEM((SLOTS, BLOCK, GROUP), BF16),
            sem((4,)), sem((8,)),
            sem((2, 7)), sem((2, 8)),
            sem((4, 10)), sem((4, 10)),
            sem((4, 7)), sem((4, 7)),
            sem((8,)), sem((8,)),
        ],
        compiler_params=pltpu.CompilerParams(
            collective_id=0, has_side_effects=True, vmem_limit_bytes=56 * 2**20
        ),
        name="causal_attention",
    )(queries, keys, values)


def solution(mesh):
    spec = P(("ctx", "head"), None)
    return jax.shard_map(per_device, mesh=mesh, in_specs=(spec, spec, spec), out_specs=spec, check_vma=False)
```

```python
import functools

import jax
import jax.numpy as jnp
from jax import lax
from jax.experimental import pallas as pl
from jax.experimental.pallas import tpu as pltpu
from jax.sharding import PartitionSpec as P

BLOCK = 128
WIDTH = 128
GROUP = 4 * WIDTH
ROWS = 4 * BLOCK
CHUNK = 1024
AHEAD = 2048
BEHIND = 512
SPAN = 256
SLOTS = 8
LOG2_SCALE = WIDTH**-0.5 * 1.4426950408889634
MESH = pl.DeviceIdType.MESH
F32 = jnp.float32
BF16 = jnp.bfloat16


def kernel(
    q_ref, k_ref, v_ref, out_ref,
    kv, kv_out, v_raw, q_in, q_pair, peak, total, acc, score_a, score_b, top_a, top_b, o_buf,
    local_sem, load_sem, own_sem, home_send, home_recv, mate_send, mate_recv, core_send, core_recv, out_send, out_recv,
):
    y = lax.axis_index("ctx")
    head = lax.axis_index("head")
    x, z, c = head // 8, lax.rem(head, 8) // 2, lax.rem(head, 2)
    low_y, low_x, low_z = (lax.min(v, 3 - v) for v in (y, x, z))
    high_y, high_x, high_z = (v // 2 for v in (y, x, z))
    my_slot = my_head = 4 * high_y + 2 * high_x + high_z
    my_chunk, my_row = 4 * high_y + high_x, 4 * c + high_z

    def at(y_, x_, z_, c_):
        return (y_, x_ * 8 + z_ * 2 + c_)

    def beside(v):
        return v + 1 - 2 * lax.rem(v, 2)

    homes = []
    for flip in range(7, 0, -1):
        y_, x_, z_ = (3 - v if flip & bit else v for v, bit in ((y, 4), (x, 2), (z, 1)))
        homes.append((4 * (y_ // 2) + 2 * (x_ // 2) + z_ // 2, at(y_, x_, z_, c)))
    mate_y, mate_x, mate_z = at(beside(y), x, z, c), at(y, beside(x), z, c), at(y, x, beside(z), c)
    twin = at(y, x, z, 1 - c)

    barrier = pltpu.get_barrier_semaphore()
    for other in [to for _, to in homes] + [mate_y, mate_x, mate_z, twin]:
        pl.semaphore_signal(barrier, inc=1, device_id=other, device_id_type=MESH)

    def columns(head_, width):
        return pl.ds(pl.multiple_of(head_ * width, width), width)

    load_v = pltpu.make_async_copy(v_ref, v_raw, local_sem.at[0])
    load_v.start()
    load_k = [
        pltpu.make_async_copy(k_ref.at[:, h * WIDTH : (h + 1) * WIDTH], kv_out.at[h, 0], load_sem.at[h]) for h in range(8)
    ]
    for copy in load_k:
        copy.start()
    own = [pltpu.make_async_copy(q_ref.at[:, columns(my_head, GROUP)], q_in.at[my_slot], local_sem.at[1])]
    own[0].start()
    peak[...] = jnp.full_like(peak, -1e30)
    total[...] = jnp.zeros_like(total)
    acc[...] = jnp.zeros_like(acc)
    pl.semaphore_wait(barrier, 11)

    home, mates, core = (home_send, home_recv), (mate_send, mate_recv), (core_send, core_recv)
    sent = {}

    def send(src, dst, sems, index, device, recv_index=None):
        send_sem, recv_sem = sems
        pltpu.make_async_remote_copy(
            src_ref=src,
            dst_ref=dst,
            send_sem=send_sem.at[index],
            recv_sem=recv_sem.at[index if recv_index is None else recv_index],
            device_id=device,
            device_id_type=MESH,
        ).start()
        sent[id(send_sem), index] = (send_sem, src.shape)

    def arrived(dst, recv_sem):
        pltpu.make_async_remote_copy(
            src_ref=dst, dst_ref=dst, send_sem=local_sem.at[0], recv_sem=recv_sem, device_id=twin, device_id_type=MESH
        ).wait_recv()

    def send_queries():
        for i, (there, to) in enumerate(homes):
            send(q_ref.at[:, columns(there, GROUP)], q_in.at[my_slot], home, (1, i), to, (1, my_slot))

    def send_kv():
        for i, (there, to) in enumerate(homes):
            send(kv_out.at[there], kv.at[my_chunk, my_row], home, (0, i), to, (0, my_slot))

    pl.when(high_y == 1)(send_queries)
    load_v.wait()
    for h in range(8):
        kv_out[h, 1] = v_raw[:, h * WIDTH : (h + 1) * WIDTH].T
    for copy in load_k:
        copy.wait()
    pl.when(high_y == 0)(send_kv)
    own.append(pltpu.make_async_copy(kv_out.at[my_head], kv.at[my_chunk, my_row], local_sem.at[2]))
    own[-1].start()
    for copy in own:
        copy.wait()

    def piece(quarter, chunk, chunks, mz, c_=c):
        return kv.at[pl.ds(4 * quarter + chunk, chunks), pl.ds(4 * c_ + 2 * mz, 2)]

    def pass_on(what, to_what, number, device):
        send(piece(*what), piece(*to_what), mates, (to_what[0], number), device)

    def to_twin(number, *what):
        send(piece(*what), piece(*what), core, (what[0], number), twin)

    def got(number, *what):
        arrived(piece(*what), mate_recv.at[what[0], number])

    def of_twin(number, *what):
        arrived(piece(*what, 1 - c), core_recv.at[what[0], number])

    def own_1(q):
        for hx in range(2):
            for hz in range(2):
                slot = 4 * q + 2 * hx + hz

                @pl.when(slot != my_slot)
                def _():
                    arrived(kv.at[4 * q + hx, 4 * c + hz], home_recv.at[0, slot])

            if hx == 0:
                pass_on((q, 0, 1, 0), (q, 2, 1, 0), 0, mate_x)
            else:
                pass_on((q, 1, 1, 0), (q, 1, 1, 1), 1, mate_z)
        to_twin(0, q, 0, 2, 0)
        pass_on((q, 1, 1, 0), (q, 3, 1, 0), 2, mate_x)
        pass_on((q, 0, 1, 0), (q, 0, 1, 1), 3, mate_z)
        pass_on((q, 0, 2, 0), (2 + q, 0, 2, 0), 0, mate_y)

    def own_2(q):
        got(0, q, 2, 1, 0)
        to_twin(1, q, 2, 1, 0)
        got(1, q, 1, 1, 1)
        to_twin(2, q, 1, 1, 1)
        pass_on((q, 2, 1, 0), (q, 2, 1, 1), 4, mate_z)
        pass_on((q, 1, 1, 1), (q, 3, 1, 1), 5, mate_x)
        pass_on((q, 2, 1, 0), (2 + q, 2, 1, 0), 1, mate_y)
        pass_on((q, 1, 1, 1), (2 + q, 1, 1, 1), 2, mate_y)

    def own_3(q):
        got(3, q, 0, 1, 1)
        to_twin(3, q, 0, 1, 1)
        got(2, q, 3, 1, 0)
        to_twin(4, q, 3, 1, 0)

    def own_4(q):
        got(4, q, 2, 1, 1)
        to_twin(5, q, 2, 1, 1)
        got(5, q, 3, 1, 1)
        to_twin(6, q, 3, 1, 1)

    def own_twin_1(q):
        of_twin(0, q, 0, 2, 0)
        of_twin(1, q, 2, 1, 0)
        of_twin(2, q, 1, 1, 1)

    def own_twin_2(q):
        for number, (chunk, mz) in enumerate(((0, 1), (3, 0), (2, 1), (3, 1))):
            of_twin(3 + number, q, chunk, 1, mz)

    def mate_1(q):
        q = 2 + q
        got(0, q, 0, 2, 0)
        pass_on((q, 0, 1, 0), (q, 0, 1, 1), 3, mate_z)
        pass_on((q, 1, 1, 0), (q, 3, 1, 0), 4, mate_x)
        to_twin(0, q, 0, 2, 0)

    def mate_2(q):
        q = 2 + q
        got(1, q, 2, 1, 0)
        pass_on((q, 2, 1, 0), (q, 2, 1, 1), 5, mate_z)
        to_twin(1, q, 2, 1, 0)
        got(2, q, 1, 1, 1)
        pass_on((q, 1, 1, 1), (q, 3, 1, 1), 6, mate_x)
        to_twin(2, q, 1, 1, 1)

    def mate_3(q):
        q = 2 + q
        for number, (chunk, mz) in enumerate(((0, 1), (3, 0), (2, 1), (3, 1))):
            got(3 + number, q, chunk, 1, mz)
            to_twin(3 + number, q, chunk, 1, mz)

    def mate_twin_1(q):
        own_twin_1(2 + q)

    def mate_twin_2(q):
        own_twin_2(2 + q)

    def split_queries(slot):
        @pl.when(slot != my_slot)
        def _():
            arrived(q_in.at[slot], home_recv.at[1, slot])

        for h in range(4):
            scaled = q_in[slot, :, h * WIDTH : (h + 1) * WIDTH].astype(F32) * LOG2_SCALE
            first = scaled.astype(BF16)
            q_pair[slot, h * BLOCK : (h + 1) * BLOCK, :WIDTH] = first
            q_pair[slot, h * BLOCK : (h + 1) * BLOCK, WIDTH:] = (scaled - first.astype(F32)).astype(BF16)

    order = []
    for z_ in range(4):
        mz = low_z if min(z_, 3 - z_) == 0 else 1 - low_z
        order += [4 * c_ + 2 * mz + z_ // 2 for c_ in range(2)]

    def in_order(*chunks):
        return [(chunk, row) for chunk in chunks for row in order]

    def parts(blocks, size):
        return [blocks[i : i + size // BLOCK] for i in range(0, len(blocks), size // BLOCK)]

    def from_pairs(pairs):
        return [(chunk, 4 * c_ + 2 * mz + hz) for chunk, mz in pairs for c_ in range(2) for hz in range(2)]

    def work(ahead, behind, after_span=None):
        ahead_parts = parts(ahead[1], AHEAD) if ahead else []
        behind_parts = parts(behind[1], BEHIND) if behind else []
        for start in range(0, ROWS, SPAN):
            columns_ = slice(start, start + SPAN)
            if behind:
                slot, _, src, src_top = behind
                old = peak[slot, :, columns_]
                new = jnp.maximum(old, jnp.max(src_top[:, columns_], axis=0, keepdims=True))
                rescale = jnp.exp2(old - new)
                peak[slot, :, columns_] = new
                sums, mixture = total[slot, :, columns_] * rescale, None
            highest = None
            for i in range(max(len(ahead_parts), len(behind_parts))):
                if i < len(ahead_parts):
                    slot_, blocks_, dst, dst_top, offset = ahead
                    k = jnp.concatenate([kv[chunk, b, 0] for chunk, b in ahead_parts[i]], axis=0)
                    rows = slice(i * AHEAD, i * AHEAD + k.shape[0])
                    s = lax.dot_general(
                        jnp.concatenate([k, k], axis=1), q_pair[slot_, columns_], (((1,), (1,)), ((), ())),
                        preferred_element_type=F32,
                    )
                    if offset is not None and rows.stop > BLOCK * len(blocks_) - CHUNK:
                        past = rows.start + CHUNK - BLOCK * len(blocks_)
                        key = past + lax.broadcasted_iota(jnp.int32, s.shape, 0)
                        token = lax.rem(lax.broadcasted_iota(jnp.int32, s.shape, 1), BLOCK)
                        s = jnp.where(key <= token + offset, s, -1e30)
                    dst[rows, columns_] = s
                    best = jnp.max(s.reshape(-1, 8, SPAN), axis=0)
                    highest = best if highest is None else jnp.maximum(highest, best)
                if i < len(behind_parts):
                    rows = slice(i * BEHIND, i * BEHIND + BLOCK * len(behind_parts[i]))
                    weights = jnp.exp2(src[rows, columns_] - new)
                    sums = sums + jnp.sum(weights.reshape(-1, 8, SPAN), axis=0)
                    v = jnp.concatenate([kv[chunk, b, 1] for chunk, b in behind_parts[i]], axis=1)
                    term = jnp.dot(v, weights.astype(BF16), preferred_element_type=F32)
                    mixture = term if mixture is None else mixture + term
            if ahead:
                dst_top[:, columns_] = highest
            if behind:
                total[slot, :, columns_] = sums
                acc[slot, :, columns_] = acc[slot, :, columns_] * rescale + mixture
                if after_span is not None:
                    after_span(slot, start // SPAN)

    def result(slot, span):
        here = (slice(None), slice(span * SPAN, (span + 1) * SPAN))
        there = (slice(None), pl.ds(pl.multiple_of(my_head * GROUP + span * SPAN, SPAN), SPAN))
        return o_buf.at[(slot, *here)], out_ref.at[there]

    def finish_span(slot, span):
        for h in range(span * SPAN // BLOCK, (span + 1) * SPAN // BLOCK):
            columns_ = slice(h * BLOCK, (h + 1) * BLOCK)
            part = acc[slot, :, columns_] * (1.0 / jnp.sum(total[slot, :, columns_], axis=0, keepdims=True))
            o_buf[slot, :, h * WIDTH : (h + 1) * WIDTH] = part.T.astype(BF16)
        src, dst = result(slot, span)

        @pl.when(slot != my_slot)
        def _():
            pltpu.make_async_remote_copy(
                src_ref=src,
                dst_ref=dst,
                send_sem=out_send.at[slot, span],
                recv_sem=out_recv.at[my_head, span],
                device_id=at(
                    low_y + slot // 4 * (3 - 2 * low_y),
                    low_x + lax.rem(slot, 4) // 2 * (3 - 2 * low_x),
                    low_z + lax.rem(slot, 2) * (3 - 2 * low_z),
                    c,
                ),
                device_id_type=MESH,
            ).start()

        @pl.when(slot == my_slot)
        def _():
            pltpu.make_async_copy(src, dst, own_sem.at[span]).start()

    def finish(slot):
        for span in range(ROWS // SPAN):
            finish_span(slot, span)

    def lower_queries(_):
        for slot in range(4):
            split_queries(slot)

    own_1(0)
    pl.when(high_y == 0)(send_queries)
    own_2(0)
    pl.when(high_y == 1)(send_kv)
    split_queries(4)
    split_queries(5)
    own_twin_1(0)

    def side_of(k):
        return lax.rem(high_z + 3 - k, 2)

    def lead_edge(r, k):
        return 4 * r + 2 + side_of(k), [(4 * r, 0), (4 * r, 1), (4 * r + 2, 0), (4 * r + 2, 1)]

    def wide_edge(r, k):
        return 4 * r + 2 * (1 - low_x) + side_of(k), in_order(4 * r + 3 - low_x, 4 * r + 1 - low_x)

    def narrow_edge(r, k):
        return 4 * r + 2 * low_x + side_of(k), in_order(4 * r + low_x)

    def offset_of(k):
        return BLOCK * (2 * (low_z + side_of(k) * (3 - 2 * low_z)) + c)

    narrow_last = lax.rem(high_x + low_x + 1, 2)

    def half_of(quarter, part):
        return [
            (4 * quarter, part),
            (4 * quarter + 1 + part, part),
            (4 * quarter + 1 + 2 * part, 1 - part),
            (4 * quarter + 2 + part, part),
        ]

    def among(r, k, m):
        upper, quarter = 1 - (1 - r) * low_y, 2 + r * (1 - low_y)
        hx = 1 - high_x if m < 2 else high_x
        return 4 * upper + 2 * hx + side_of(k), half_of(quarter, m % 2)

    def pick(first, one, other):
        (slot, pairs), (slot_, pairs_) = one, other
        return jnp.where(first, slot, slot_), [
            tuple(jnp.where(first, v, w) for v, w in zip(p, p_, strict=True)) for p, p_ in zip(pairs, pairs_, strict=True)
        ]

    def unit(r, j):
        past = j - (8 - 8 * r)
        later = pick(past < 2, lead_edge(r, past), among(r, 0, 0))
        return pick(past < 0, (4 + lax.rem(j, 4), half_of(0, lax.rem(j, 8) // 4)), later)

    def whole(one):
        return one[0], from_pairs(one[1])

    steps = {
        1: [(split_queries, 7), (mate_1, 0), (own_4, 0)],
        2: [(mate_2, 0)],
        3: [(lower_queries, 0), (own_1, 1)],
        4: [(mate_3, 0), (mate_twin_1, 0)],
        5: [(mate_twin_1, 1)],
    }
    halfway = {0: [(split_queries, 6), (own_3, 0)], 1: [(own_twin_2, 0)], 5: [(mate_3, 1)]}
    places = {
        (0, 0, 0): [(mate_twin_2, 0)],
        (0, 0, 3): [(own_2, 1)],
        (0, 1, 0): [(own_3, 1), (mate_1, 1)],
        (0, 1, 1): [(own_4, 1), (mate_2, 1)],
        (0, 1, 2): [(own_twin_1, 1), (own_twin_2, 1)],
        (1, 0, 0): [(mate_twin_2, 1)],
    }

    def do(actions):
        def run():
            for action, quarter in actions:
                action(quarter)

        return run

    a, b = (score_a, top_a), (score_b, top_b)
    zero = jnp.int32(0)
    work((*whole(unit(zero, zero)), *a, None), None)

    def full(r, i, _):
        for step, actions in steps.items():
            pl.when(i + 5 * r == step)(do(actions))
        work((*whole(unit(r, 2 * i + 1)), *b, None), (*whole(unit(r, 2 * i)), *a))
        for step, actions in halfway.items():
            pl.when(i + 5 * r == step)(do(actions))
        work((*whole(unit(r, 2 * i + 2)), *a, None), (*whole(unit(r, 2 * i + 1)), *b))
        return 0

    def slots(r, k, _):
        def at_place(number):
            for (r_, k_, number_), actions in places.items():
                if number_ == number:
                    pl.when((r == r_) & (k == k_))(do(actions))

        offset = offset_of(k)
        edges = narrow_edge(r, k), wide_edge(r, k)
        after = whole(pick(k == 0, among(r, 1, 0), lead_edge(1, 0)))
        fills = [whole(among(r, k, m)) for m in range(4)]

        def visit(one, two):
            at_place(0)
            work((*fills[1], *b, None), (*fills[0], *a))
            at_place(3)
            work((*one, *a, offset), (*fills[1], *b))
            work((*fills[2], *b, None), (*one, *a))
            finish(one[0])
            at_place(1)
            work((*fills[3], *a, None), (*fills[2], *b))
            work((*two, *b, offset), (*fills[3], *a))
            at_place(2)
            pl.when(r + k < 2)(lambda: work((*after, *a, None), (*two, *b)))
            pl.when(r + k < 2)(lambda: finish(two[0]))
            pl.when(r + k == 2)(lambda: work(None, (*two, *b), finish_span))

        pl.when(narrow_last == 0)(lambda: visit(*edges))
        pl.when(narrow_last == 1)(lambda: visit(*edges[::-1]))
        return 0

    def round_(r, _):
        lax.fori_loop(0, 5 - 4 * r, functools.partial(full, r), 0)
        lax.fori_loop(0, 2, functools.partial(slots, r), 0)
        return 0

    lax.fori_loop(0, 2, round_, 0)

    for (_, index), (send_sem, shape) in sent.items():
        held = {
            (BLOCK, GROUP): q_in.at[0],
            (2, BLOCK, WIDTH): kv.at[0, 0],
            (1, 2, 2, BLOCK, WIDTH): kv.at[pl.ds(0, 1), pl.ds(0, 2)],
            (2, 2, 2, BLOCK, WIDTH): kv.at[pl.ds(0, 2), pl.ds(0, 2)],
        }[shape]
        pltpu.make_async_remote_copy(
            src_ref=held, dst_ref=held, send_sem=send_sem.at[index], recv_sem=local_sem.at[0], device_id=twin,
            device_id_type=MESH,
        ).wait_send()
    for slot in range(SLOTS):
        for span in range(ROWS // SPAN):
            src, dst = result(slot, span)

            @pl.when(slot != my_slot)
            def _():
                done = pltpu.make_async_remote_copy(
                    src_ref=src,
                    dst_ref=out_ref.at[:, pl.ds(slot * GROUP + span * SPAN, SPAN)],
                    send_sem=out_send.at[slot, span],
                    recv_sem=out_recv.at[slot, span],
                    device_id=twin,
                    device_id_type=MESH,
                )
                done.wait_send()
                done.wait_recv()

            @pl.when(slot == my_slot)
            def _():
                pltpu.make_async_copy(src, dst, own_sem.at[span]).wait()


def per_device(queries, keys, values):
    sem = pltpu.SemaphoreType.DMA
    return pl.pallas_call(
        kernel,
        out_shape=pltpu.VMEM(queries.shape, BF16),
        in_specs=[pl.BlockSpec(memory_space=pl.ANY)] * 3,
        out_specs=pl.BlockSpec(memory_space=pltpu.VMEM),
        scratch_shapes=[
            pltpu.VMEM((16, 8, 2, BLOCK, WIDTH), BF16),
            pltpu.VMEM((8, 2, BLOCK, WIDTH), BF16),
            pltpu.VMEM((BLOCK, 8 * WIDTH), BF16),
            pltpu.VMEM((SLOTS, BLOCK, GROUP), BF16),
            pltpu.VMEM((SLOTS, ROWS, 2 * WIDTH), BF16),
            pltpu.VMEM((SLOTS, 1, ROWS), F32),
            pltpu.VMEM((SLOTS, 8, ROWS), F32),
            pltpu.VMEM((SLOTS, WIDTH, ROWS), F32),
            pltpu.VMEM((2 * CHUNK, ROWS), F32),
            pltpu.VMEM((2 * CHUNK, ROWS), F32),
            pltpu.VMEM((8, ROWS), F32),
            pltpu.VMEM((8, ROWS), F32),
            pltpu.VMEM((SLOTS, BLOCK, GROUP), BF16),
            sem((4,)), sem((8,)), sem((2,)),
            sem((2, 7)), sem((2, 8)),
            sem((4, 7)), sem((4, 7)),
            sem((4, 7)), sem((4, 7)),
            sem((8, 2)), sem((8, 2)),
        ],
        compiler_params=pltpu.CompilerParams(
            collective_id=0, has_side_effects=True, vmem_limit_bytes=56 * 2**20
        ),
        name="causal_attention",
    )(queries, keys, values)


def solution(mesh):
    spec = P(("ctx", "head"), None)
    return jax.shard_map(per_device, mesh=mesh, in_specs=(spec, spec, spec), out_specs=spec, check_vma=False)
```

```python
import functools

import jax
import jax.numpy as jnp
from jax import lax
from jax.experimental import pallas as pl
from jax.experimental.pallas import tpu as pltpu
from jax.sharding import PartitionSpec as P

BLOCK = 128
WIDTH = 128
GROUP = 4 * WIDTH
ROWS = 4 * BLOCK
CHUNK = 1024
AHEAD = 2048
BEHIND = 512
SPAN = 256
SLOTS = 8
LOG2_SCALE = WIDTH**-0.5 * 1.4426950408889634
MESH = pl.DeviceIdType.MESH
F32 = jnp.float32
BF16 = jnp.bfloat16


def kernel(
    q_ref, k_ref, v_ref, out_ref,
    kv, kv_out, v_raw, q_in, q_pair, peak, total, acc, score_a, score_b, top_a, top_b, o_buf,
    local_sem, load_sem, own_sem, home_send, home_recv, mate_send, mate_recv, core_send, core_recv, out_send, out_recv,
):
    y = lax.axis_index("ctx")
    head = lax.axis_index("head")
    x, z, c = head // 8, lax.rem(head, 8) // 2, lax.rem(head, 2)
    low_y, low_x, low_z = (lax.min(v, 3 - v) for v in (y, x, z))
    high_y, high_x, high_z = (v // 2 for v in (y, x, z))
    my_slot = my_head = 4 * high_y + 2 * high_x + high_z
    my_chunk, my_row = 4 * high_y + high_x, 4 * c + high_z

    def at(y_, x_, z_, c_):
        return (y_, x_ * 8 + z_ * 2 + c_)

    def beside(v):
        return v + 1 - 2 * lax.rem(v, 2)

    homes = []
    for flip in range(7, 0, -1):
        y_, x_, z_ = (3 - v if flip & bit else v for v, bit in ((y, 4), (x, 2), (z, 1)))
        homes.append((4 * (y_ // 2) + 2 * (x_ // 2) + z_ // 2, at(y_, x_, z_, c)))
    mate_y, mate_x, mate_z = at(beside(y), x, z, c), at(y, beside(x), z, c), at(y, x, beside(z), c)
    twin = at(y, x, z, 1 - c)

    barrier = pltpu.get_barrier_semaphore()
    for other in [to for _, to in homes] + [mate_y, mate_x, mate_z, twin]:
        pl.semaphore_signal(barrier, inc=1, device_id=other, device_id_type=MESH)

    def columns(head_, width):
        return pl.ds(pl.multiple_of(head_ * width, width), width)

    load_v = pltpu.make_async_copy(v_ref, v_raw, local_sem.at[0])
    load_v.start()
    load_k = [
        pltpu.make_async_copy(k_ref.at[:, h * WIDTH : (h + 1) * WIDTH], kv_out.at[h, 0], load_sem.at[h]) for h in range(8)
    ]
    for copy in load_k:
        copy.start()
    own = [pltpu.make_async_copy(q_ref.at[:, columns(my_head, GROUP)], q_in.at[my_slot], local_sem.at[1])]
    own[0].start()
    peak[...] = jnp.full_like(peak, -1e30)
    total[...] = jnp.zeros_like(total)
    acc[...] = jnp.zeros_like(acc)
    pl.semaphore_wait(barrier, 11)

    home, mates, core = (home_send, home_recv), (mate_send, mate_recv), (core_send, core_recv)
    sent = {}

    def send(src, dst, sems, index, device, recv_index=None):
        send_sem, recv_sem = sems
        pltpu.make_async_remote_copy(
            src_ref=src,
            dst_ref=dst,
            send_sem=send_sem.at[index],
            recv_sem=recv_sem.at[index if recv_index is None else recv_index],
            device_id=device,
            device_id_type=MESH,
        ).start()
        sent[id(send_sem), index] = (send_sem, src.shape)

    def arrived(dst, recv_sem):
        pltpu.make_async_remote_copy(
            src_ref=dst, dst_ref=dst, send_sem=local_sem.at[0], recv_sem=recv_sem, device_id=twin, device_id_type=MESH
        ).wait_recv()

    def send_queries():
        for i, (there, to) in enumerate(homes):
            send(q_ref.at[:, columns(there, GROUP)], q_in.at[my_slot], home, (1, i), to, (1, my_slot))

    def send_kv():
        for i, (there, to) in enumerate(homes):
            send(kv_out.at[there], kv.at[my_chunk, my_row], home, (0, i), to, (0, my_slot))

    pl.when(high_y == 1)(send_queries)
    load_v.wait()
    for h in range(8):
        kv_out[h, 1] = v_raw[:, h * WIDTH : (h + 1) * WIDTH].T
    for copy in load_k:
        copy.wait()
    pl.when(high_y == 0)(send_kv)
    own.append(pltpu.make_async_copy(kv_out.at[my_head], kv.at[my_chunk, my_row], local_sem.at[2]))
    own[-1].start()
    for copy in own:
        copy.wait()

    def piece(quarter, chunk, chunks, mz, c_=c):
        return kv.at[pl.ds(4 * quarter + chunk, chunks), pl.ds(4 * c_ + 2 * mz, 2)]

    def pass_on(what, to_what, number, device):
        send(piece(*what), piece(*to_what), mates, (to_what[0], number), device)

    def to_twin(number, *what):
        send(piece(*what), piece(*what), core, (what[0], number), twin)

    def got(number, *what):
        arrived(piece(*what), mate_recv.at[what[0], number])

    def of_twin(number, *what):
        arrived(piece(*what, 1 - c), core_recv.at[what[0], number])

    def own_1(q):
        for hx in range(2):
            for hz in range(2):
                slot = 4 * q + 2 * hx + hz

                @pl.when(slot != my_slot)
                def _():
                    arrived(kv.at[4 * q + hx, 4 * c + hz], home_recv.at[0, slot])

            if hx == 0:
                pass_on((q, 0, 1, 0), (q, 2, 1, 0), 0, mate_x)
            else:
                pass_on((q, 1, 1, 0), (q, 1, 1, 1), 1, mate_z)
        to_twin(0, q, 0, 2, 0)
        pass_on((q, 1, 1, 0), (q, 3, 1, 0), 2, mate_x)
        pass_on((q, 0, 1, 0), (q, 0, 1, 1), 3, mate_z)
        pass_on((q, 0, 2, 0), (2 + q, 0, 2, 0), 0, mate_y)

    def own_2(q):
        got(0, q, 2, 1, 0)
        to_twin(1, q, 2, 1, 0)
        got(1, q, 1, 1, 1)
        to_twin(2, q, 1, 1, 1)
        pass_on((q, 2, 1, 0), (q, 2, 1, 1), 4, mate_z)
        pass_on((q, 1, 1, 1), (q, 3, 1, 1), 5, mate_x)
        pass_on((q, 2, 1, 0), (2 + q, 2, 1, 0), 1, mate_y)
        pass_on((q, 1, 1, 1), (2 + q, 1, 1, 1), 2, mate_y)

    def own_3(q):
        got(3, q, 0, 1, 1)
        to_twin(3, q, 0, 1, 1)
        got(2, q, 3, 1, 0)
        to_twin(4, q, 3, 1, 0)

    def own_4(q):
        got(4, q, 2, 1, 1)
        to_twin(5, q, 2, 1, 1)
        got(5, q, 3, 1, 1)
        to_twin(6, q, 3, 1, 1)

    def own_twin_1(q):
        of_twin(0, q, 0, 2, 0)
        of_twin(1, q, 2, 1, 0)
        of_twin(2, q, 1, 1, 1)

    def own_twin_2(q):
        for number, (chunk, mz) in enumerate(((0, 1), (3, 0), (2, 1), (3, 1))):
            of_twin(3 + number, q, chunk, 1, mz)

    def mate_1(q):
        q = 2 + q
        got(0, q, 0, 2, 0)
        pass_on((q, 0, 1, 0), (q, 0, 1, 1), 3, mate_z)
        pass_on((q, 1, 1, 0), (q, 3, 1, 0), 4, mate_x)
        to_twin(0, q, 0, 2, 0)

    def mate_2(q):
        q = 2 + q
        got(1, q, 2, 1, 0)
        pass_on((q, 2, 1, 0), (q, 2, 1, 1), 5, mate_z)
        to_twin(1, q, 2, 1, 0)
        got(2, q, 1, 1, 1)
        pass_on((q, 1, 1, 1), (q, 3, 1, 1), 6, mate_x)
        to_twin(2, q, 1, 1, 1)

    def mate_3(q):
        q = 2 + q
        for number, (chunk, mz) in enumerate(((0, 1), (3, 0), (2, 1), (3, 1))):
            got(3 + number, q, chunk, 1, mz)
            to_twin(3 + number, q, chunk, 1, mz)

    def mate_twin_1(q):
        own_twin_1(2 + q)

    def mate_twin_2(q):
        own_twin_2(2 + q)

    def split_queries(slot):
        @pl.when(slot != my_slot)
        def _():
            arrived(q_in.at[slot], home_recv.at[1, slot])

        for h in range(4):
            scaled = q_in[slot, :, h * WIDTH : (h + 1) * WIDTH].astype(F32) * LOG2_SCALE
            first = scaled.astype(BF16)
            q_pair[slot, h * BLOCK : (h + 1) * BLOCK, :WIDTH] = first
            q_pair[slot, h * BLOCK : (h + 1) * BLOCK, WIDTH:] = (scaled - first.astype(F32)).astype(BF16)

    order = []
    for z_ in range(4):
        mz = low_z if min(z_, 3 - z_) == 0 else 1 - low_z
        order += [4 * c_ + 2 * mz + z_ // 2 for c_ in range(2)]

    def in_order(*chunks):
        return [(chunk, row) for chunk in chunks for row in order]

    def parts(blocks, size):
        return [blocks[i : i + size // BLOCK] for i in range(0, len(blocks), size // BLOCK)]

    def from_pairs(pairs):
        return [(chunk, 4 * c_ + 2 * mz + hz) for chunk, mz in pairs for c_ in range(2) for hz in range(2)]

    def work(ahead, behind, after_span=None):
        ahead_parts = parts(ahead[1], AHEAD) if ahead else []
        behind_parts = parts(behind[1], BEHIND) if behind else []
        for start in range(0, ROWS, SPAN):
            columns_ = slice(start, start + SPAN)
            if behind:
                slot, _, src, src_top = behind
                old = peak[slot, :, columns_]
                new = jnp.maximum(old, jnp.max(src_top[:, columns_], axis=0, keepdims=True))
                rescale = jnp.exp2(old - new)
                peak[slot, :, columns_] = new
                sums, mixture = total[slot, :, columns_] * rescale, None
            highest = None
            for i in range(max(len(ahead_parts), len(behind_parts))):
                if i < len(ahead_parts):
                    slot_, blocks_, dst, dst_top, offset = ahead
                    k = jnp.concatenate([kv[chunk, b, 0] for chunk, b in ahead_parts[i]], axis=0)
                    rows = slice(i * AHEAD, i * AHEAD + k.shape[0])
                    s = lax.dot_general(
                        jnp.concatenate([k, k], axis=1), q_pair[slot_, columns_], (((1,), (1,)), ((), ())),
                        preferred_element_type=F32,
                    )
                    if offset is not None and rows.stop > BLOCK * len(blocks_) - CHUNK:
                        past = rows.start + CHUNK - BLOCK * len(blocks_)
                        key = past + lax.broadcasted_iota(jnp.int32, s.shape, 0)
                        token = lax.rem(lax.broadcasted_iota(jnp.int32, s.shape, 1), BLOCK)
                        s = jnp.where(key <= token + offset, s, -1e30)
                    dst[rows, columns_] = s
                    best = jnp.max(s.reshape(-1, 8, SPAN), axis=0)
                    highest = best if highest is None else jnp.maximum(highest, best)
                if i < len(behind_parts):
                    rows = slice(i * BEHIND, i * BEHIND + BLOCK * len(behind_parts[i]))
                    weights = jnp.exp2(src[rows, columns_] - new)
                    sums = sums + jnp.sum(weights.reshape(-1, 8, SPAN), axis=0)
                    v = jnp.concatenate([kv[chunk, b, 1] for chunk, b in behind_parts[i]], axis=1)
                    term = jnp.dot(v, weights.astype(BF16), preferred_element_type=F32)
                    mixture = term if mixture is None else mixture + term
            if ahead:
                dst_top[:, columns_] = highest
            if behind:
                total[slot, :, columns_] = sums
                acc[slot, :, columns_] = acc[slot, :, columns_] * rescale + mixture
                if after_span is not None:
                    after_span(slot, start // SPAN)

    def result(slot, span):
        here = (slice(None), slice(span * SPAN, (span + 1) * SPAN))
        there = (slice(None), pl.ds(pl.multiple_of(my_head * GROUP + span * SPAN, SPAN), SPAN))
        return o_buf.at[(slot, *here)], out_ref.at[there]

    def finish_span(slot, span):
        for h in range(span * SPAN // BLOCK, (span + 1) * SPAN // BLOCK):
            columns_ = slice(h * BLOCK, (h + 1) * BLOCK)
            part = acc[slot, :, columns_] * (1.0 / jnp.sum(total[slot, :, columns_], axis=0, keepdims=True))
            o_buf[slot, :, h * WIDTH : (h + 1) * WIDTH] = part.T.astype(BF16)
        src, dst = result(slot, span)

        @pl.when(slot != my_slot)
        def _():
            pltpu.make_async_remote_copy(
                src_ref=src,
                dst_ref=dst,
                send_sem=out_send.at[slot, span],
                recv_sem=out_recv.at[my_head, span],
                device_id=at(
                    low_y + slot // 4 * (3 - 2 * low_y),
                    low_x + lax.rem(slot, 4) // 2 * (3 - 2 * low_x),
                    low_z + lax.rem(slot, 2) * (3 - 2 * low_z),
                    c,
                ),
                device_id_type=MESH,
            ).start()

        @pl.when(slot == my_slot)
        def _():
            pltpu.make_async_copy(src, dst, own_sem.at[span]).start()

    def finish(slot):
        for span in range(ROWS // SPAN):
            finish_span(slot, span)

    def lower_queries(_):
        for slot in range(4):
            split_queries(slot)

    own_1(0)
    pl.when(high_y == 0)(send_queries)
    own_2(0)
    pl.when(high_y == 1)(send_kv)
    split_queries(4)
    split_queries(5)
    own_twin_1(0)

    def side_of(k):
        return lax.rem(high_z + 3 - k, 2)

    def lead_edge(r, k):
        return 4 * r + 2 + side_of(k), [(4 * r, 0), (4 * r, 1), (4 * r + 2, 0), (4 * r + 2, 1)]

    def wide_edge(r, k):
        return 4 * r + 2 * (1 - low_x) + side_of(k), in_order(4 * r + 3 - low_x, 4 * r + 1 - low_x)

    def narrow_edge(r, k):
        return 4 * r + 2 * low_x + side_of(k), in_order(4 * r + low_x)

    def offset_of(k):
        return BLOCK * (2 * (low_z + side_of(k) * (3 - 2 * low_z)) + c)

    narrow_last = lax.rem(high_x + low_x + 1, 2)

    def half_of(quarter, part):
        return [
            (4 * quarter, part),
            (4 * quarter + 1 + part, part),
            (4 * quarter + 1 + 2 * part, 1 - part),
            (4 * quarter + 2 + part, part),
        ]

    def among(r, k, m):
        upper, quarter = 1 - (1 - r) * low_y, 2 + r * (1 - low_y)
        hx = 1 - high_x if m < 2 else high_x
        return 4 * upper + 2 * hx + side_of(k), half_of(quarter, m % 2)

    def pick(first, one, other):
        (slot, pairs), (slot_, pairs_) = one, other
        return jnp.where(first, slot, slot_), [
            tuple(jnp.where(first, v, w) for v, w in zip(p, p_, strict=True)) for p, p_ in zip(pairs, pairs_, strict=True)
        ]

    def unit(r, j):
        past = j - (8 - 8 * r)
        later = pick(past < 2, lead_edge(r, past), among(r, 0, 0))
        return pick(past < 0, (4 + lax.rem(j, 4), half_of(0, lax.rem(j, 8) // 4)), later)

    def whole(one):
        return one[0], from_pairs(one[1])

    steps = {
        1: [(split_queries, 7), (mate_1, 0), (own_4, 0)],
        2: [(mate_2, 0), (own_1, 1)],
        4: [(mate_3, 0), (mate_twin_1, 0)],
        5: [(mate_twin_1, 1)],
    }
    halfway = {
        0: [(split_queries, 6), (own_3, 0)],
        1: [(own_twin_2, 0)],
        3: [(lower_queries, 0)],
    }
    places = {
        (0, 0, 0): [(mate_twin_2, 0), (own_2, 1)],
        (0, 0, 1): [(own_3, 1), (mate_1, 1)],
        (0, 1, 0): [(own_4, 1)],
        (0, 1, 3): [(mate_2, 1)],
        (0, 1, 2): [(own_twin_1, 1), (own_twin_2, 1), (mate_3, 1)],
        (1, 0, 0): [(mate_twin_2, 1)],
    }

    def do(actions):
        def run():
            for action, quarter in actions:
                action(quarter)

        return run

    a, b = (score_a, top_a), (score_b, top_b)
    zero = jnp.int32(0)
    work((*whole(unit(zero, zero)), *a, None), None)

    def full(r, i, _):
        for step, actions in steps.items():
            pl.when(i + 5 * r == step)(do(actions))
        work((*whole(unit(r, 2 * i + 1)), *b, None), (*whole(unit(r, 2 * i)), *a))
        for step, actions in halfway.items():
            pl.when(i + 5 * r == step)(do(actions))
        work((*whole(unit(r, 2 * i + 2)), *a, None), (*whole(unit(r, 2 * i + 1)), *b))
        return 0

    def slots(r, k, _):
        def at_place(number):
            for (r_, k_, number_), actions in places.items():
                if number_ == number:
                    pl.when((r == r_) & (k == k_))(do(actions))

        offset = offset_of(k)
        edges = narrow_edge(r, k), wide_edge(r, k)
        after = whole(pick(k == 0, among(r, 1, 0), lead_edge(1, 0)))
        fills = [whole(among(r, k, m)) for m in range(4)]

        def visit(one, two):
            at_place(0)
            work((*fills[1], *b, None), (*fills[0], *a))
            at_place(3)
            work((*one, *a, offset), (*fills[1], *b))
            work((*fills[2], *b, None), (*one, *a))
            finish(one[0])
            at_place(1)
            work((*fills[3], *a, None), (*fills[2], *b))
            work((*two, *b, offset), (*fills[3], *a))
            at_place(2)
            pl.when(r + k < 2)(lambda: work((*after, *a, None), (*two, *b)))
            pl.when(r + k < 2)(lambda: finish(two[0]))
            pl.when(r + k == 2)(lambda: work(None, (*two, *b), finish_span))

        pl.when(narrow_last == 0)(lambda: visit(*edges))
        pl.when(narrow_last == 1)(lambda: visit(*edges[::-1]))
        return 0

    def round_(r, _):
        lax.fori_loop(0, 5 - 4 * r, functools.partial(full, r), 0)
        lax.fori_loop(0, 2, functools.partial(slots, r), 0)
        return 0

    lax.fori_loop(0, 2, round_, 0)

    for (_, index), (send_sem, shape) in sent.items():
        held = {
            (BLOCK, GROUP): q_in.at[0],
            (2, BLOCK, WIDTH): kv.at[0, 0],
            (1, 2, 2, BLOCK, WIDTH): kv.at[pl.ds(0, 1), pl.ds(0, 2)],
            (2, 2, 2, BLOCK, WIDTH): kv.at[pl.ds(0, 2), pl.ds(0, 2)],
        }[shape]
        pltpu.make_async_remote_copy(
            src_ref=held, dst_ref=held, send_sem=send_sem.at[index], recv_sem=local_sem.at[0], device_id=twin,
            device_id_type=MESH,
        ).wait_send()
    for slot in range(SLOTS):
        for span in range(ROWS // SPAN):
            src, dst = result(slot, span)

            @pl.when(slot != my_slot)
            def _():
                done = pltpu.make_async_remote_copy(
                    src_ref=src,
                    dst_ref=out_ref.at[:, pl.ds(slot * GROUP + span * SPAN, SPAN)],
                    send_sem=out_send.at[slot, span],
                    recv_sem=out_recv.at[slot, span],
                    device_id=twin,
                    device_id_type=MESH,
                )
                done.wait_send()
                done.wait_recv()

            @pl.when(slot == my_slot)
            def _():
                pltpu.make_async_copy(src, dst, own_sem.at[span]).wait()


def per_device(queries, keys, values):
    sem = pltpu.SemaphoreType.DMA
    return pl.pallas_call(
        kernel,
        out_shape=pltpu.VMEM(queries.shape, BF16),
        in_specs=[pl.BlockSpec(memory_space=pl.ANY)] * 3,
        out_specs=pl.BlockSpec(memory_space=pltpu.VMEM),
        scratch_shapes=[
            pltpu.VMEM((16, 8, 2, BLOCK, WIDTH), BF16),
            pltpu.VMEM((8, 2, BLOCK, WIDTH), BF16),
            pltpu.VMEM((BLOCK, 8 * WIDTH), BF16),
            pltpu.VMEM((SLOTS, BLOCK, GROUP), BF16),
            pltpu.VMEM((SLOTS, ROWS, 2 * WIDTH), BF16),
            pltpu.VMEM((SLOTS, 1, ROWS), F32),
            pltpu.VMEM((SLOTS, 8, ROWS), F32),
            pltpu.VMEM((SLOTS, WIDTH, ROWS), F32),
            pltpu.VMEM((2 * CHUNK, ROWS), F32),
            pltpu.VMEM((2 * CHUNK, ROWS), F32),
            pltpu.VMEM((8, ROWS), F32),
            pltpu.VMEM((8, ROWS), F32),
            pltpu.VMEM((SLOTS, BLOCK, GROUP), BF16),
            sem((4,)), sem((8,)), sem((2,)),
            sem((2, 7)), sem((2, 8)),
            sem((4, 7)), sem((4, 7)),
            sem((4, 7)), sem((4, 7)),
            sem((8, 2)), sem((8, 2)),
        ],
        compiler_params=pltpu.CompilerParams(
            collective_id=0, has_side_effects=True, vmem_limit_bytes=56 * 2**20
        ),
        name="causal_attention",
    )(queries, keys, values)


def solution(mesh):
    spec = P(("ctx", "head"), None)
    return jax.shard_map(per_device, mesh=mesh, in_specs=(spec, spec, spec), out_specs=spec, check_vma=False)
```

```python
import functools

import jax
import jax.numpy as jnp
from jax import lax
from jax.experimental import pallas as pl
from jax.experimental.pallas import tpu as pltpu
from jax.sharding import PartitionSpec as P

BLOCK = 128
WIDTH = 128
GROUP = 4 * WIDTH
ROWS = 4 * BLOCK
CHUNK = 1024
AHEAD = 2048
BEHIND = 512
SPAN = 256
SLOTS = 8
LOG2_SCALE = WIDTH**-0.5 * 1.4426950408889634
MESH = pl.DeviceIdType.MESH
F32 = jnp.float32
BF16 = jnp.bfloat16


def kernel(
    q_ref, k_ref, v_ref, out_ref,
    kv, kv_out, v_raw, q_in, q_pair, peak, total, acc, score_a, score_b, top_a, top_b, o_buf,
    local_sem, load_sem, own_sem, home_send, home_recv, mate_send, mate_recv, core_send, core_recv, out_send, out_recv,
):
    y = lax.axis_index("ctx")
    head = lax.axis_index("head")
    x, z, c = head // 8, lax.rem(head, 8) // 2, lax.rem(head, 2)
    low_y, low_x, low_z = (lax.min(v, 3 - v) for v in (y, x, z))
    high_y, high_x, high_z = (v // 2 for v in (y, x, z))
    my_slot = my_head = 4 * high_y + 2 * high_x + high_z
    my_chunk, my_row = 4 * high_y + high_x, 4 * c + high_z

    def at(y_, x_, z_, c_):
        return (y_, x_ * 8 + z_ * 2 + c_)

    def beside(v):
        return v + 1 - 2 * lax.rem(v, 2)

    homes = []
    for flip in range(7, 0, -1):
        y_, x_, z_ = (3 - v if flip & bit else v for v, bit in ((y, 4), (x, 2), (z, 1)))
        homes.append((4 * (y_ // 2) + 2 * (x_ // 2) + z_ // 2, at(y_, x_, z_, c)))
    mate_y, mate_x, mate_z = at(beside(y), x, z, c), at(y, beside(x), z, c), at(y, x, beside(z), c)
    twin = at(y, x, z, 1 - c)

    barrier = pltpu.get_barrier_semaphore()
    for other in [to for _, to in homes] + [mate_y, mate_x, mate_z, twin]:
        pl.semaphore_signal(barrier, inc=1, device_id=other, device_id_type=MESH)

    def columns(head_, width):
        return pl.ds(pl.multiple_of(head_ * width, width), width)

    load_v = pltpu.make_async_copy(v_ref, v_raw, local_sem.at[0])
    load_v.start()
    load_k = [
        pltpu.make_async_copy(k_ref.at[:, h * WIDTH : (h + 1) * WIDTH], kv_out.at[h, 0], load_sem.at[h]) for h in range(8)
    ]
    for copy in load_k:
        copy.start()
    own = [pltpu.make_async_copy(q_ref.at[:, columns(my_head, GROUP)], q_in.at[my_slot], local_sem.at[1])]
    own[0].start()
    peak[...] = jnp.full_like(peak, -1e30)
    total[...] = jnp.zeros_like(total)
    acc[...] = jnp.zeros_like(acc)
    pl.semaphore_wait(barrier, 11)

    home, mates, core = (home_send, home_recv), (mate_send, mate_recv), (core_send, core_recv)
    sent = {}

    def send(src, dst, sems, index, device, recv_index=None):
        send_sem, recv_sem = sems
        pltpu.make_async_remote_copy(
            src_ref=src,
            dst_ref=dst,
            send_sem=send_sem.at[index],
            recv_sem=recv_sem.at[index if recv_index is None else recv_index],
            device_id=device,
            device_id_type=MESH,
        ).start()
        sent[id(send_sem), index] = (send_sem, src.shape)

    def arrived(dst, recv_sem):
        pltpu.make_async_remote_copy(
            src_ref=dst, dst_ref=dst, send_sem=local_sem.at[0], recv_sem=recv_sem, device_id=twin, device_id_type=MESH
        ).wait_recv()

    def send_queries():
        for i, (there, to) in enumerate(homes):
            send(q_ref.at[:, columns(there, GROUP)], q_in.at[my_slot], home, (1, i), to, (1, my_slot))

    def send_kv():
        for i, (there, to) in enumerate(homes):
            send(kv_out.at[there], kv.at[my_chunk, my_row], home, (0, i), to, (0, my_slot))

    pl.when(high_y == 1)(send_queries)
    load_v.wait()
    for h in range(8):
        kv_out[h, 1] = v_raw[:, h * WIDTH : (h + 1) * WIDTH].T
    for copy in load_k:
        copy.wait()
    pl.when(high_y == 0)(send_kv)
    own.append(pltpu.make_async_copy(kv_out.at[my_head], kv.at[my_chunk, my_row], local_sem.at[2]))
    own[-1].start()
    for copy in own:
        copy.wait()

    def piece(quarter, chunk, chunks, mz, c_=c):
        return kv.at[pl.ds(4 * quarter + chunk, chunks), pl.ds(4 * c_ + 2 * mz, 2)]

    def pass_on(what, to_what, number, device):
        send(piece(*what), piece(*to_what), mates, (to_what[0], number), device)

    def to_twin(number, *what):
        send(piece(*what), piece(*what), core, (what[0], number), twin)

    def got(number, *what):
        arrived(piece(*what), mate_recv.at[what[0], number])

    def of_twin(number, *what):
        arrived(piece(*what, 1 - c), core_recv.at[what[0], number])

    def own_1(q):
        for hx in range(2):
            for hz in range(2):
                slot = 4 * q + 2 * hx + hz

                @pl.when(slot != my_slot)
                def _():
                    arrived(kv.at[4 * q + hx, 4 * c + hz], home_recv.at[0, slot])

            if hx == 0:
                pass_on((q, 0, 1, 0), (q, 2, 1, 0), 0, mate_x)
            else:
                pass_on((q, 1, 1, 0), (q, 1, 1, 1), 1, mate_z)
        to_twin(0, q, 0, 2, 0)
        pass_on((q, 1, 1, 0), (q, 3, 1, 0), 2, mate_x)
        pass_on((q, 0, 1, 0), (q, 0, 1, 1), 3, mate_z)
        pass_on((q, 0, 2, 0), (2 + q, 0, 2, 0), 0, mate_y)

    def own_2(q):
        got(0, q, 2, 1, 0)
        to_twin(1, q, 2, 1, 0)
        got(1, q, 1, 1, 1)
        to_twin(2, q, 1, 1, 1)
        pass_on((q, 2, 1, 0), (q, 2, 1, 1), 4, mate_z)
        pass_on((q, 1, 1, 1), (q, 3, 1, 1), 5, mate_x)
        pass_on((q, 2, 1, 0), (2 + q, 2, 1, 0), 1, mate_y)
        pass_on((q, 1, 1, 1), (2 + q, 1, 1, 1), 2, mate_y)

    def own_3(q):
        got(3, q, 0, 1, 1)
        to_twin(3, q, 0, 1, 1)
        got(2, q, 3, 1, 0)
        to_twin(4, q, 3, 1, 0)

    def own_4(q):
        got(4, q, 2, 1, 1)
        to_twin(5, q, 2, 1, 1)
        got(5, q, 3, 1, 1)
        to_twin(6, q, 3, 1, 1)

    def own_twin_1(q):
        of_twin(0, q, 0, 2, 0)
        of_twin(1, q, 2, 1, 0)
        of_twin(2, q, 1, 1, 1)

    def own_twin_2(q):
        for number, (chunk, mz) in enumerate(((0, 1), (3, 0), (2, 1), (3, 1))):
            of_twin(3 + number, q, chunk, 1, mz)

    def mate_1(q):
        q = 2 + q
        got(0, q, 0, 2, 0)
        pass_on((q, 0, 1, 0), (q, 0, 1, 1), 3, mate_z)
        pass_on((q, 1, 1, 0), (q, 3, 1, 0), 4, mate_x)
        to_twin(0, q, 0, 2, 0)

    def mate_2(q):
        q = 2 + q
        got(1, q, 2, 1, 0)
        pass_on((q, 2, 1, 0), (q, 2, 1, 1), 5, mate_z)
        to_twin(1, q, 2, 1, 0)
        got(2, q, 1, 1, 1)
        pass_on((q, 1, 1, 1), (q, 3, 1, 1), 6, mate_x)
        to_twin(2, q, 1, 1, 1)

    def mate_3(q):
        q = 2 + q
        for number, (chunk, mz) in enumerate(((0, 1), (3, 0), (2, 1), (3, 1))):
            got(3 + number, q, chunk, 1, mz)
            to_twin(3 + number, q, chunk, 1, mz)

    def mate_twin_1(q):
        own_twin_1(2 + q)

    def mate_twin_2(q):
        own_twin_2(2 + q)

    def split_queries(slot):
        @pl.when(slot != my_slot)
        def _():
            arrived(q_in.at[slot], home_recv.at[1, slot])

        for h in range(4):
            scaled = q_in[slot, :, h * WIDTH : (h + 1) * WIDTH].astype(F32) * LOG2_SCALE
            first = scaled.astype(BF16)
            q_pair[slot, h * BLOCK : (h + 1) * BLOCK, :WIDTH] = first
            q_pair[slot, h * BLOCK : (h + 1) * BLOCK, WIDTH:] = (scaled - first.astype(F32)).astype(BF16)

    order = []
    for z_ in range(4):
        mz = low_z if min(z_, 3 - z_) == 0 else 1 - low_z
        order += [4 * c_ + 2 * mz + z_ // 2 for c_ in range(2)]

    def in_order(*chunks):
        return [(chunk, row) for chunk in chunks for row in order]

    def parts(blocks, size):
        return [blocks[i : i + size // BLOCK] for i in range(0, len(blocks), size // BLOCK)]

    def from_pairs(pairs):
        return [(chunk, 4 * c_ + 2 * mz + hz) for c_ in (c, 1 - c) for chunk, mz in pairs for hz in range(2)]

    def work(ahead, behind, after_span=None):
        ahead_parts = parts(ahead[1], AHEAD) if ahead else []
        behind_parts = parts(behind[1], BEHIND) if behind else []
        for start in range(0, ROWS, SPAN):
            columns_ = slice(start, start + SPAN)
            if behind:
                slot, _, src, src_top = behind
                old = peak[slot, :, columns_]
                new = jnp.maximum(old, jnp.max(src_top[:, columns_], axis=0, keepdims=True))
                rescale = jnp.exp2(old - new)
                peak[slot, :, columns_] = new
                sums, mixture = total[slot, :, columns_] * rescale, None
            highest = None
            for i in range(max(len(ahead_parts), len(behind_parts))):
                if i < len(ahead_parts):
                    slot_, blocks_, dst, dst_top, offset = ahead
                    k = jnp.concatenate([kv[chunk, b, 0] for chunk, b in ahead_parts[i]], axis=0)
                    rows = slice(i * AHEAD, i * AHEAD + k.shape[0])
                    s = lax.dot_general(
                        jnp.concatenate([k, k], axis=1), q_pair[slot_, columns_], (((1,), (1,)), ((), ())),
                        preferred_element_type=F32,
                    )
                    if offset is not None and rows.stop > BLOCK * len(blocks_) - CHUNK:
                        past = rows.start + CHUNK - BLOCK * len(blocks_)
                        key = past + lax.broadcasted_iota(jnp.int32, s.shape, 0)
                        token = lax.rem(lax.broadcasted_iota(jnp.int32, s.shape, 1), BLOCK)
                        s = jnp.where(key <= token + offset, s, -1e30)
                    dst[rows, columns_] = s
                    best = jnp.max(s.reshape(-1, 8, SPAN), axis=0)
                    highest = best if highest is None else jnp.maximum(highest, best)
                if i < len(behind_parts):
                    rows = slice(i * BEHIND, i * BEHIND + BLOCK * len(behind_parts[i]))
                    weights = jnp.exp2(src[rows, columns_] - new)
                    sums = sums + jnp.sum(weights.reshape(-1, 8, SPAN), axis=0)
                    v = jnp.concatenate([kv[chunk, b, 1] for chunk, b in behind_parts[i]], axis=1)
                    term = jnp.dot(v, weights.astype(BF16), preferred_element_type=F32)
                    mixture = term if mixture is None else mixture + term
            if ahead:
                dst_top[:, columns_] = highest
            if behind:
                total[slot, :, columns_] = sums
                acc[slot, :, columns_] = acc[slot, :, columns_] * rescale + mixture
                if after_span is not None:
                    after_span(slot, start // SPAN)

    def result(slot, span):
        here = (slice(None), slice(span * SPAN, (span + 1) * SPAN))
        there = (slice(None), pl.ds(pl.multiple_of(my_head * GROUP + span * SPAN, SPAN), SPAN))
        return o_buf.at[(slot, *here)], out_ref.at[there]

    def finish_span(slot, span):
        for h in range(span * SPAN // BLOCK, (span + 1) * SPAN // BLOCK):
            columns_ = slice(h * BLOCK, (h + 1) * BLOCK)
            part = acc[slot, :, columns_] * (1.0 / jnp.sum(total[slot, :, columns_], axis=0, keepdims=True))
            o_buf[slot, :, h * WIDTH : (h + 1) * WIDTH] = part.astype(BF16).T
        src, dst = result(slot, span)

        @pl.when(slot != my_slot)
        def _():
            pltpu.make_async_remote_copy(
                src_ref=src,
                dst_ref=dst,
                send_sem=out_send.at[slot, span],
                recv_sem=out_recv.at[my_head, span],
                device_id=at(
                    low_y + slot // 4 * (3 - 2 * low_y),
                    low_x + lax.rem(slot, 4) // 2 * (3 - 2 * low_x),
                    low_z + lax.rem(slot, 2) * (3 - 2 * low_z),
                    c,
                ),
                device_id_type=MESH,
            ).start()

        @pl.when(slot == my_slot)
        def _():
            pltpu.make_async_copy(src, dst, own_sem.at[span]).start()

    def finish(slot):
        for span in range(ROWS // SPAN):
            finish_span(slot, span)

    def lower_queries(_):
        for slot in range(4):
            split_queries(slot)

    own_1(0)
    pl.when(high_y == 0)(send_queries)
    own_2(0)
    pl.when(high_y == 1)(send_kv)
    split_queries(4)
    split_queries(5)

    def side_of(k):
        return lax.rem(high_z + 3 - k, 2)

    def lead_edge(r, k):
        return 4 * r + 2 + side_of(k), [(4 * r, 0), (4 * r, 1), (4 * r + 2, 0), (4 * r + 2, 1)]

    def wide_edge(r, k):
        return 4 * r + 2 * (1 - low_x) + side_of(k), in_order(4 * r + 3 - low_x, 4 * r + 1 - low_x)

    def narrow_edge(r, k):
        return 4 * r + 2 * low_x + side_of(k), in_order(4 * r + low_x)

    def offset_of(k):
        return BLOCK * (2 * (low_z + side_of(k) * (3 - 2 * low_z)) + c)

    narrow_last = lax.rem(high_x + low_x + 1, 2)

    def half_of(quarter, part):
        return [
            (4 * quarter, part),
            (4 * quarter + 1 + part, part),
            (4 * quarter + 1 + 2 * part, 1 - part),
            (4 * quarter + 2 + part, part),
        ]

    def among(r, k, m):
        upper, quarter = 1 - (1 - r) * low_y, 2 + r * (1 - low_y)
        hx = 1 - high_x if m < 2 else high_x
        return 4 * upper + 2 * hx + side_of(k), half_of(quarter, m % 2)

    def pick(first, one, other):
        (slot, pairs), (slot_, pairs_) = one, other
        return jnp.where(first, slot, slot_), [
            tuple(jnp.where(first, v, w) for v, w in zip(p, p_, strict=True)) for p, p_ in zip(pairs, pairs_, strict=True)
        ]

    def unit(r, j):
        past = j - (8 - 8 * r)
        later = pick(past < 2, lead_edge(r, past), among(r, 0, 0))
        return pick(past < 0, (4 + lax.rem(j, 4), half_of(0, lax.rem(j, 8) // 4)), later)

    def whole(one):
        return one[0], from_pairs(one[1])

    steps = {
        1: [(split_queries, 7), (mate_1, 0), (own_4, 0)],
        2: [(mate_2, 0), (own_1, 1)],
        4: [(mate_3, 0), (mate_twin_1, 0)],
        5: [(mate_twin_1, 1)],
    }
    halfway = {
        0: [(split_queries, 6), (own_3, 0)],
        1: [(own_twin_2, 0)],
        3: [(lower_queries, 0)],
    }
    places = {
        (0, 0, 0): [(mate_twin_2, 0), (own_2, 1)],
        (0, 0, 1): [(own_3, 1), (mate_1, 1)],
        (0, 1, 0): [(own_4, 1)],
        (0, 1, 3): [(mate_2, 1)],
        (0, 1, 2): [(own_twin_1, 1), (own_twin_2, 1), (mate_3, 1)],
        (1, 0, 0): [(mate_twin_2, 1)],
    }

    def do(actions):
        def run():
            for action, quarter in actions:
                action(quarter)

        return run

    a, b = (score_a, top_a), (score_b, top_b)
    zero = jnp.int32(0)
    slot_0, blocks_0 = whole(unit(zero, zero))
    for part in range(2):
        if part == 1:
            own_twin_1(0)
        keys_0 = jnp.concatenate([kv[chunk, row, 0] for chunk, row in blocks_0[8 * part : 8 * part + 8]], axis=0)
        keys_0 = jnp.concatenate([keys_0, keys_0], axis=1)
        for start in range(0, ROWS, SPAN):
            columns_0 = slice(start, start + SPAN)
            s_0 = lax.dot_general(keys_0, q_pair[slot_0, columns_0], (((1,), (1,)), ((), ())), preferred_element_type=F32)
            score_a[CHUNK * part : CHUNK * (part + 1), columns_0] = s_0
            best = jnp.max(s_0.reshape(-1, 8, SPAN), axis=0)
            top_a[:, columns_0] = jnp.maximum(top_a[:, columns_0], best) if part else best

    def full(r, i, _):
        for step, actions in steps.items():
            pl.when(i + 5 * r == step)(do(actions))
        work((*whole(unit(r, 2 * i + 1)), *b, None), (*whole(unit(r, 2 * i)), *a))
        for step, actions in halfway.items():
            pl.when(i + 5 * r == step)(do(actions))
        work((*whole(unit(r, 2 * i + 2)), *a, None), (*whole(unit(r, 2 * i + 1)), *b))
        return 0

    def slots(r, k, _):
        def at_place(number):
            for (r_, k_, number_), actions in places.items():
                if number_ == number:
                    pl.when((r == r_) & (k == k_))(do(actions))

        offset = offset_of(k)
        edges = narrow_edge(r, k), wide_edge(r, k)
        after = whole(pick(k == 0, among(r, 1, 0), lead_edge(1, 0)))
        fills = [whole(among(r, k, m)) for m in range(4)]

        def visit(one, two):
            at_place(0)
            work((*fills[1], *b, None), (*fills[0], *a))
            at_place(3)
            work((*one, *a, offset), (*fills[1], *b))
            work((*fills[2], *b, None), (*one, *a))
            finish(one[0])
            at_place(1)
            work((*fills[3], *a, None), (*fills[2], *b))
            work((*two, *b, offset), (*fills[3], *a))
            at_place(2)
            pl.when(r + k < 2)(lambda: work((*after, *a, None), (*two, *b)))
            pl.when(r + k < 2)(lambda: finish(two[0]))
            pl.when(r + k == 2)(lambda: work(None, (*two, *b), finish_span))

        pl.when(narrow_last == 0)(lambda: visit(*edges))
        pl.when(narrow_last == 1)(lambda: visit(*edges[::-1]))
        return 0

    def round_(r, _):
        lax.fori_loop(0, 5 - 4 * r, functools.partial(full, r), 0)
        lax.fori_loop(0, 2, functools.partial(slots, r), 0)
        return 0

    lax.fori_loop(0, 2, round_, 0)

    for (_, index), (send_sem, shape) in sent.items():
        held = {
            (BLOCK, GROUP): q_in.at[0],
            (2, BLOCK, WIDTH): kv.at[0, 0],
            (1, 2, 2, BLOCK, WIDTH): kv.at[pl.ds(0, 1), pl.ds(0, 2)],
            (2, 2, 2, BLOCK, WIDTH): kv.at[pl.ds(0, 2), pl.ds(0, 2)],
        }[shape]
        pltpu.make_async_remote_copy(
            src_ref=held, dst_ref=held, send_sem=send_sem.at[index], recv_sem=local_sem.at[0], device_id=twin,
            device_id_type=MESH,
        ).wait_send()
    for slot in range(SLOTS):
        for span in range(ROWS // SPAN):
            src, dst = result(slot, span)

            @pl.when(slot != my_slot)
            def _():
                done = pltpu.make_async_remote_copy(
                    src_ref=src,
                    dst_ref=out_ref.at[:, pl.ds(slot * GROUP + span * SPAN, SPAN)],
                    send_sem=out_send.at[slot, span],
                    recv_sem=out_recv.at[slot, span],
                    device_id=twin,
                    device_id_type=MESH,
                )
                done.wait_send()
                done.wait_recv()

            @pl.when(slot == my_slot)
            def _():
                pltpu.make_async_copy(src, dst, own_sem.at[span]).wait()


def per_device(queries, keys, values):
    sem = pltpu.SemaphoreType.DMA
    return pl.pallas_call(
        kernel,
        out_shape=pltpu.VMEM(queries.shape, BF16),
        in_specs=[pl.BlockSpec(memory_space=pl.ANY)] * 3,
        out_specs=pl.BlockSpec(memory_space=pltpu.VMEM),
        scratch_shapes=[
            pltpu.VMEM((16, 8, 2, BLOCK, WIDTH), BF16),
            pltpu.VMEM((8, 2, BLOCK, WIDTH), BF16),
            pltpu.VMEM((BLOCK, 8 * WIDTH), BF16),
            pltpu.VMEM((SLOTS, BLOCK, GROUP), BF16),
            pltpu.VMEM((SLOTS, ROWS, 2 * WIDTH), BF16),
            pltpu.VMEM((SLOTS, 1, ROWS), F32),
            pltpu.VMEM((SLOTS, 8, ROWS), F32),
            pltpu.VMEM((SLOTS, WIDTH, ROWS), F32),
            pltpu.VMEM((2 * CHUNK, ROWS), F32),
            pltpu.VMEM((2 * CHUNK, ROWS), F32),
            pltpu.VMEM((8, ROWS), F32),
            pltpu.VMEM((8, ROWS), F32),
            pltpu.VMEM((SLOTS, BLOCK, GROUP), BF16),
            sem((4,)), sem((8,)), sem((2,)),
            sem((2, 7)), sem((2, 8)),
            sem((4, 7)), sem((4, 7)),
            sem((4, 7)), sem((4, 7)),
            sem((8, 2)), sem((8, 2)),
        ],
        compiler_params=pltpu.CompilerParams(
            collective_id=0, has_side_effects=True, vmem_limit_bytes=56 * 2**20
        ),
        name="causal_attention",
    )(queries, keys, values)


def solution(mesh):
    spec = P(("ctx", "head"), None)
    return jax.shard_map(per_device, mesh=mesh, in_specs=(spec, spec, spec), out_specs=spec, check_vma=False)
```
